32 devices in a mesh: dp: 4 (over z), seq: 8 (over y, x, core).
Axes of the slice: x: 2, y: 2, z: 4, core: 2. Of those that a mesh axis runs over, the one named last changes fastest.
Arguments:
- latents: bfloat16 [8, 4096, 1152], P('dp', 'seq'), may hold values from -56 to 56
- out_grad: bfloat16 [8, 4096, 1152], P('dp', 'seq'), may hold values from -6 to 6
- phrases: bfloat16 [8, 32, 1152], P('dp'), may hold values from -6 to 6
- query_weight: bfloat16 [1152, 1152], replicated, may hold values from -0.1875 to 0.1875
- key_weight: bfloat16 [1152, 1152], P('seq'), may hold values from -0.1875 to 0.1875
- value_weight: bfloat16 [1152, 1152], P('seq'), may hold values from -0.1875 to 0.1875
- first_weight: bfloat16 [1152, 1152], P('seq'), may hold values from -0.1875 to 0.1875
- second_weight: bfloat16 [1152, 1152], P('seq'), may hold values from -0.1875 to 0.1875
- region_first: int32 [8, 32], P('dp'), may hold values from 0 to 31, as said below
- region_last: int32 [8, 32], P('dp'), may hold values from 0 to 31
- phrase_counts: int32 [8], P('dp'), may hold values from 8 to 32, as said below
Outputs:
- latent_grad: bfloat16 [8, 4096, 1152], P('dp', 'seq')
- phrase_grad: bfloat16 [8, 32, 1152], P('dp')
- first_grad: float32 [1152, 1152], P('seq')
- second_grad: float32 [1152, 1152], P('seq')
The draws below stay inside these ranges and needn't reach their ends.
Inputs may be any that keep to these rules, and one draw needn't show every extreme that they name: region_first <= region_last for every phrase; phrase 0 of every image covers all 32 blocks. Slots from phrase_counts on are padding.
All inputs are finite; a program needn't handle non-finite values.
Results may differ from the reference program's by a relative error of at most 0.015.
The reference program's roundings to bfloat16 on the way (of `hidden`, `encoded`, `queries`, `probs_low`, `score_grad`, `query_grad`, `encoded_grad` and `act_grad`) count: a program that leaves them out, or rounds other values in their place, can miss the bound.
Values may be sent and summed in bfloat16 or wider, within the bound.
No kernel may reach another device: no remote copies, remote signals or barrier semaphores. Data moves between devices by JAX's collectives and lax.ppermute only.
A program may use at most 128 MiB of HBM per device.

```python
import jax
import jax.numpy as jnp
from jax import lax

D = 1152
H = 16
HD = 72
P_SIZE = 32
BLOCK = 128
NBLK = 32
TOKENS = 4096
IMAGES = 8


def region_bounds(key):
    base_key = jax.random.fold_in(key, 41)
    start_key, span_key = jax.random.split(base_key)
    region_first = jax.random.randint(start_key, (IMAGES, P_SIZE), 0, NBLK, dtype=jnp.int32)
    levels = NBLK.bit_length()
    exponent = jax.random.randint(span_key, (IMAGES, P_SIZE), 0, levels, dtype=jnp.int32)
    span_len = jnp.left_shift(jnp.ones((IMAGES, P_SIZE), jnp.int32), exponent)
    region_last = jnp.minimum(region_first + span_len - 1, NBLK - 1)
    region_first = region_first.at[:, 0].set(0)
    region_last = region_last.at[:, 0].set(NBLK - 1)
    return (region_first, region_last)


def draw_region_first(key, part):
    return region_bounds(key)[0]


def draw_region_last(key, part):
    return region_bounds(key)[1]


def draw_phrase_counts(key, part):
    drawn = jax.random.randint(jax.random.fold_in(key, 43), (IMAGES,), P_SIZE // 4, P_SIZE + 1, dtype=jnp.int32)
    return drawn.at[0].set(P_SIZE)


def draw_latents(key, part):
    normal_key = jax.random.fold_in(jax.random.fold_in(key, 47), 0)
    drawn = jnp.clip(jax.random.normal(normal_key, (IMAGES, TOKENS, D), jnp.float32), -6.0, 6.0)
    return drawn.astype(jnp.bfloat16)


def block_scale(own_key, shape, cuts, low, largest):
    gain, own = 1.0, jax.random.fold_in(own_key, 6)
    for dim, parts in cuts:
        draws = jnp.exp(jax.random.uniform(jax.random.fold_in(own, dim), (parts,), jnp.float32, low / len(cuts), largest / len(cuts)))
        gain = gain * jnp.repeat(draws, shape[dim] // parts).reshape([-1 if axis == dim else 1 for axis in range(len(shape))])
    return gain


def gaussian(key, shape, scale, limit, shards=(), kind=jnp.bfloat16):
    gain = block_scale(key, shape, shards, -0.22, 0.18) if shards else 1.0
    result = jax.random.normal(key, shape, jnp.float32) * scale * gain
    return jnp.minimum(jnp.maximum(result, -limit), limit).astype(kind)


def setup_inputs(seed: int = 0) -> dict:
    keys = jax.random.split(jax.random.key(seed), 12)
    latents = draw_latents(jax.random.fold_in(keys[11], 71), 0)
    out_grad = gaussian(keys[1], (IMAGES, TOKENS, D), 1.0, 6.0, ((0, 4), (1, 8)))
    phrases = gaussian(keys[2], (IMAGES, P_SIZE, D), 1.0, 6.0, ((0, 4),))
    query_weight = gaussian(keys[3], (D, D), D ** -0.5, 0.1875)
    key_weight = gaussian(keys[4], (D, D), D ** -0.5, 0.1875, ((0, 8),))
    value_weight = gaussian(keys[5], (D, D), D ** -0.5, 0.1875, ((0, 8),))
    first_weight = gaussian(keys[6], (D, D), D ** -0.5, 0.1875, ((0, 8),))
    second_weight = gaussian(keys[7], (D, D), D ** -0.5, 0.1875, ((0, 8),))
    region_first = draw_region_first(jax.random.fold_in(keys[11], 71), 0)
    region_last = draw_region_last(jax.random.fold_in(keys[11], 71), 0)
    phrase_counts = draw_phrase_counts(jax.random.fold_in(keys[11], 71), 0)
    return {"latents": latents, "out_grad": out_grad, "phrases": phrases, "query_weight": query_weight, "key_weight": key_weight, "value_weight": value_weight, "first_weight": first_weight, "second_weight": second_weight, "region_first": region_first, "region_last": region_last, "phrase_counts": phrase_counts}


def silu_slope(pre_act):
    sigmoid = jax.nn.sigmoid(pre_act)
    return sigmoid * (1.0 + pre_act * (1.0 - sigmoid))


def reference(latents, out_grad, phrases, query_weight, key_weight, value_weight, first_weight, second_weight, region_first, region_last, phrase_counts):
    score_scale = HD ** -0.5
    phrase_rows = phrases.reshape(IMAGES * P_SIZE, D)
    pre_act = jnp.dot(phrase_rows, first_weight, preferred_element_type=jnp.float32)
    hidden = jax.nn.silu(pre_act).astype(jnp.bfloat16)
    encoded = jnp.dot(hidden, second_weight, preferred_element_type=jnp.float32).astype(jnp.bfloat16)
    key_rows = jnp.dot(encoded, key_weight, preferred_element_type=jnp.float32).astype(jnp.bfloat16)
    value_rows = jnp.dot(encoded, value_weight, preferred_element_type=jnp.float32).astype(jnp.bfloat16)
    block_ids = jnp.arange(TOKENS, dtype=jnp.int32) // BLOCK
    phrase_ids = jnp.arange(P_SIZE, dtype=jnp.int32)
    best = lax.Precision.HIGHEST

    def one_image(inputs):
        image_latents, image_grad, image_keys, image_values, first_block, last_block, count = inputs
        queries = jnp.dot(image_latents, query_weight, preferred_element_type=jnp.float32).astype(jnp.bfloat16)
        query_heads = queries.reshape(TOKENS, H, HD).astype(jnp.float32)
        key_heads = image_keys.reshape(P_SIZE, H, HD).astype(jnp.float32)
        value_heads = image_values.reshape(P_SIZE, H, HD).astype(jnp.float32)
        grad_heads = image_grad.reshape(TOKENS, H, HD).astype(jnp.float32)
        scores = jnp.einsum("thd,phd->thp", query_heads, key_heads, precision=best) * score_scale
        visible = (phrase_ids[None, :] < count) & (first_block[None, :] <= block_ids[:, None]) & (block_ids[:, None] <= last_block[None, :])
        scores = jnp.where(visible[:, None, :], scores, -jnp.inf)
        row_max = jnp.max(scores, axis=-1, keepdims=True)
        exponent = jnp.exp(scores - row_max)
        attn_probs = exponent / jnp.sum(exponent, axis=-1, keepdims=True)
        probs_low = attn_probs.astype(jnp.bfloat16)
        prob_grad = jnp.einsum("thd,phd->thp", grad_heads, value_heads, precision=best)
        inner_sum = jnp.sum(attn_probs * prob_grad, axis=-1, keepdims=True)
        score_grad = (attn_probs * (prob_grad - inner_sum) * score_scale).astype(jnp.bfloat16)
        score_wide = score_grad.astype(jnp.float32)
        query_grad = jnp.einsum("thp,phd->thd", score_wide, key_heads, precision=best).astype(jnp.bfloat16).reshape(TOKENS, D)
        latent_grad = jnp.dot(query_grad, query_weight.T, preferred_element_type=jnp.float32).astype(jnp.bfloat16)
        key_grad = jnp.einsum("thp,thd->phd", score_wide, query_heads, precision=best).reshape(P_SIZE, D)
        value_grad = jnp.einsum("thp,thd->phd", probs_low.astype(jnp.float32), grad_heads, precision=best).reshape(P_SIZE, D)
        return latent_grad, key_grad, value_grad

    latent_grad, key_grad, value_grad = lax.map(one_image, (latents, out_grad, key_rows.reshape(IMAGES, P_SIZE, D), value_rows.reshape(IMAGES, P_SIZE, D), region_first, region_last, phrase_counts))
    key_low = key_grad.reshape(IMAGES * P_SIZE, D).astype(jnp.bfloat16)
    value_low = value_grad.reshape(IMAGES * P_SIZE, D).astype(jnp.bfloat16)
    encoded_grad = (jnp.dot(key_low, key_weight.T, preferred_element_type=jnp.float32) + jnp.dot(value_low, value_weight.T, preferred_element_type=jnp.float32)).astype(jnp.bfloat16)
    second_grad = jnp.dot(hidden.T, encoded_grad, preferred_element_type=jnp.float32)
    hidden_grad = jnp.dot(encoded_grad, second_weight.T, preferred_element_type=jnp.float32)
    act_grad = (hidden_grad * silu_slope(pre_act)).astype(jnp.bfloat16)
    first_grad = jnp.dot(phrase_rows.T, act_grad, preferred_element_type=jnp.float32)
    phrase_grad = jnp.dot(act_grad, first_weight.T, preferred_element_type=jnp.float32).astype(jnp.bfloat16).reshape(IMAGES, P_SIZE, D)
    return latent_grad, phrase_grad, first_grad, second_grad
```

```python
import functools

import jax
import jax.numpy as jnp
from jax import lax
from jax.experimental import pallas as pl
from jax.experimental.pallas import tpu as pltpu
from jax.sharding import PartitionSpec as P

H = 16
BLOCK = 128
GROUP = 8
VMEM = pl.BlockSpec(memory_space=pltpu.VMEM)
SMEM = pl.BlockSpec(memory_space=pltpu.SMEM)
ANY = pl.BlockSpec(memory_space=pl.ANY)
HBM = pl.BlockSpec(memory_space=pltpu.HBM)


def vmem(mebibytes):
    return pltpu.CompilerParams(vmem_limit_bytes=mebibytes * 1024 * 1024)


def silu_slope(pre_act):
    sigmoid = jax.nn.sigmoid(pre_act)
    return sigmoid * (1.0 + pre_act * (1.0 - sigmoid))


def contract(left_arg, right_arg, left_dim, right_dim):
    return lax.dot_general(
        left_arg,
        right_arg,
        (((left_dim,), (right_dim,)), ((), ())),
        preferred_element_type=jnp.float32,
    )


def times_transposed(left_arg, right_arg):
    return contract(left_arg, right_arg, 1, 1)


def transposed_times(left_arg, right_arg):
    return contract(left_arg, right_arg, 0, 0)


def split_times_transposed(left_arg, right_arg):
    rows = left_arg.shape[0]
    high = left_arg.astype(jnp.bfloat16)
    low = (left_arg - high.astype(jnp.float32)).astype(jnp.bfloat16)
    product = times_transposed(jnp.concatenate([high, low], axis=0), right_arg)
    return product[:rows] + product[rows:]


def visible_bias(region_first, region_last, phrase_counts, offset, tokens):
    block_ids = (offset + jnp.arange(tokens, dtype=jnp.int32)) // BLOCK
    phrase_ids = jnp.arange(region_first.shape[1], dtype=jnp.int32)
    visible = (
        (phrase_ids[None, :, None] < phrase_counts[:, None, None])
        & (region_first[:, :, None] <= block_ids[None, None, :])
        & (block_ids[None, None, :] <= region_last[:, :, None])
    )
    return jnp.where(visible, 0.0, -jnp.inf).astype(jnp.float32)


def window(group, head_size):
    start = group * GROUP * head_size
    return start // 128 * 128, -(-(start + GROUP * head_size) // 128) * 128


def own_columns(rows, group, head, head_size, low):
    first = (group * GROUP + head) * head_size - low
    column = lax.broadcasted_iota(jnp.int32, rows.shape, 1)
    return jnp.where((column >= first) & (column < first + head_size), rows, jnp.zeros_like(rows))


def block_diagonal(rows, group, head_size, low):
    return jnp.concatenate(
        [own_columns(rows, group, head, head_size, low) for head in range(GROUP)], axis=0
    )


def block_places(place_ref, scheme, chips):
    chip, core, odd = place_ref[0], place_ref[1], place_ref[2]
    steps = list(range(chips))
    if chips == 4:
        turn = odd if scheme == 0 else 1 - odd
        steps = [0, 1 + turn, 2 - turn, 3]
    return [2 * (chip ^ step) + other for other in (core, 1 - core) for step in steps]


def load_blocks(blocks, offsets, whole, places, sem):
    rows = whole.shape[0] // len(blocks)
    copies = [
        pltpu.make_async_copy(
            block.at[pl.ds(offset, rows)],
            whole.at[pl.ds(pl.multiple_of(place * rows, 16), rows)],
            sem.at[i],
        )
        for i, (block, offset, place) in enumerate(zip(blocks, offsets, places))
    ]
    for copy in copies:
        copy.start()
    return copies


def load_weight(name, layout, arrays, place_ref, chips, whole, sem):
    scheme, blocks = layout[name]
    return load_blocks(
        [arrays[array] for array, _ in blocks],
        [offset for _, offset in blocks],
        whole,
        block_places(place_ref, scheme, chips),
        sem,
    )


def project(left_arg, right_arg):
    return jnp.dot(left_arg, right_arg, preferred_element_type=jnp.float32)


def join_kernel(*refs):
    outs = [ref for ref in refs if ref.shape[0] == max(r.shape[0] for r in refs)]
    parts = iter(refs[: len(refs) - len(outs)])
    for out in outs:
        start = 0
        while start < out.shape[0]:
            part = next(parts)
            stop = min(start + part.shape[0], out.shape[0])
            out[start:stop] = part[: stop - start]
            start = stop


def join_halves(out_ref, core, start, mine, far):
    half = mine[0].shape[0]
    for plane in range(len(mine)):
        first = start + plane * 2 * half
        out_ref[pl.ds(pl.multiple_of(first + core * half, 16), half)] = mine[plane][...]
        out_ref[pl.ds(pl.multiple_of(first + (1 - core) * half, 16), half)] = far[plane][...]


def head_parts(slots):
    return [slice(head * slots, (head + 1) * slots) for head in range(GROUP)]


def own_head_sum(full, group, head_size, low):
    slots = full.shape[0] // GROUP
    return functools.reduce(
        jnp.add,
        [
            own_columns(full[part], group, head, head_size, low)
            for head, part in enumerate(head_parts(slots))
        ],
    )


def attend_kernel(chips, planes, images, layout, place_ref, phrase_ref, *refs):
    others = planes - 1
    mine, far = refs[:others], refs[others : 2 * others]
    arrays = refs[2 * others : 2 * others + layout["arrays"]]
    (
        query_ref,
        grad_ref,
        bias_ref,
        key_out,
        score_out,
        mine_out,
        other_out,
        slope_out,
        hidden_out,
        phrase_out,
        first_weight,
        second_weight,
        key_weight,
        value_weight,
        query,
        grad,
        slope,
        hidden,
        all_phrases,
        all_scores,
        value_rows,
        key_sum,
        value_sum,
        total,
        first_sem,
        second_sem,
        key_sem,
        value_sem,
        row_sem,
        out_sem,
    ) = refs[2 * others + layout["arrays"] :]
    first_copies = load_weight("first", layout, arrays, place_ref, chips, first_weight, first_sem)
    second_copies = load_weight(
        "second", layout, arrays, place_ref, chips, second_weight, second_sem
    )
    key_copies = load_weight("key", layout, arrays, place_ref, chips, key_weight, key_sem)
    value_copies = load_weight("value", layout, arrays, place_ref, chips, value_weight, value_sem)
    query_copy = pltpu.make_async_copy(query_ref, query, row_sem.at[0])
    query_copy.start()
    grad_copy = pltpu.make_async_copy(grad_ref, grad, row_sem.at[1])
    grad_copy.start()
    own_rows = phrase_ref.shape[0]
    all_phrases[:own_rows] = phrase_ref[...]
    join_halves(all_phrases, place_ref[1], own_rows, mine, far)
    out_copies = [pltpu.make_async_copy(all_phrases, phrase_out, out_sem.at[0])]
    out_copies[0].start()
    for copy in first_copies:
        copy.wait()
    pre_act = project(all_phrases[...], first_weight[...])
    sigmoid = jax.nn.sigmoid(pre_act)
    hidden[...] = (pre_act * sigmoid).astype(jnp.bfloat16)
    slope[...] = sigmoid * (1.0 + pre_act * (1.0 - sigmoid))
    out_copies.append(pltpu.make_async_copy(hidden, hidden_out, out_sem.at[1]))
    out_copies.append(pltpu.make_async_copy(slope, slope_out, out_sem.at[2]))
    out_copies[1].start()
    out_copies[2].start()
    for copy in second_copies:
        copy.wait()
    encoded = project(hidden[:own_rows], second_weight[...]).astype(jnp.bfloat16)
    for copy in key_copies:
        copy.wait()
    key_out[...] = project(encoded, key_weight[...]).astype(jnp.bfloat16)
    for copy in value_copies:
        copy.wait()
    value_rows[...] = project(encoded, value_weight[...]).astype(jnp.bfloat16)
    query_copy.wait()
    grad_copy.wait()

    slots = own_rows // images
    features = query.shape[1]
    tokens = query.shape[0] // images
    head_size = features // H
    scale = head_size ** (-0.5)
    key_sum[...] = jnp.zeros_like(key_sum)
    value_sum[...] = jnp.zeros_like(value_sum)
    for image in range(images):
        rows = pl.ds(image * slots, slots)
        here = pl.ds(image * tokens, tokens)
        bias = bias_ref[image]
        for group in range(H // GROUP):
            low, high = window(group, head_size)
            columns = pl.ds(low, high - low)
            keys = block_diagonal(key_out[rows, columns], group, head_size, low)
            values = block_diagonal(value_rows[rows, columns], group, head_size, low)
            queries = query[here, columns]
            grads = grad[here, columns]
            scores = times_transposed(keys, queries)
            prob_grad = times_transposed(values, grads)
            probs_low, score_grad = [], []
            for part in head_parts(slots):
                score = scores[part] * scale + bias
                exponent = jnp.exp(score - jnp.max(score, axis=0, keepdims=True))
                probs = exponent * (1.0 / jnp.sum(exponent, axis=0, keepdims=True))
                upstream = prob_grad[part]
                inner = jnp.sum(probs * upstream, axis=0, keepdims=True)
                probs_low.append(probs.astype(jnp.bfloat16))
                score_grad.append((probs * (upstream - inner) * scale).astype(jnp.bfloat16))
            probs_low = jnp.concatenate(probs_low, axis=0)
            score_grad = jnp.concatenate(score_grad, axis=0)
            all_scores[image, pl.ds(group * GROUP * slots, GROUP * slots)] = score_grad
            key_sum[rows, columns] += own_head_sum(
                project(score_grad, queries), group, head_size, low
            )
            value_sum[rows, columns] += own_head_sum(
                project(probs_low, grads), group, head_size, low
            )
        out_copies.append(
            pltpu.make_async_copy(all_scores.at[image], score_out.at[image], out_sem.at[3 + image])
        )
        out_copies[-1].start()
    total[...] = split_times_transposed(key_sum[...], key_weight[...]) + split_times_transposed(
        value_sum[...], value_weight[...]
    )
    core = place_ref[1]
    half = mine_out.shape[0]
    mine_out[...] = total[pl.ds(pl.multiple_of(core * half, 8), half)]
    other_out[...] = total[pl.ds(pl.multiple_of((1 - core) * half, 8), half)]
    for copy in out_copies:
        copy.wait()


def latent_kernel(score_ref, key_ref, weight_ref, out_ref, query_grad):
    features = weight_ref.shape[1]
    head_size = features // H
    slots = key_ref.shape[0]

    @pl.when(pl.program_id(0) == 0)
    def _():
        parts = []
        for group in range(H // GROUP):
            low, high = window(group, head_size)
            keys = block_diagonal(key_ref[:, low:high], group, head_size, low)
            score_grad = score_ref[0, group * GROUP * slots : (group + 1) * GROUP * slots]
            part = transposed_times(score_grad, keys)
            if low:
                part = jnp.concatenate([jnp.zeros((part.shape[0], low), jnp.float32), part], axis=1)
            if high < features:
                part = jnp.concatenate(
                    [part, jnp.zeros((part.shape[0], features - high), jnp.float32)], axis=1
                )
            parts.append(part)
        query_grad[...] = functools.reduce(jnp.add, parts).astype(jnp.bfloat16)

    out_ref[...] = times_transposed(query_grad[...], weight_ref[...]).astype(jnp.bfloat16)


def weight_grad_kernel(chips, planes, layout, place_ref, *refs):
    mine, far = refs[:planes], refs[planes : 2 * planes]
    arrays = refs[2 * planes : 2 * planes + layout["arrays"]]
    (
        slope_ref,
        hidden_ref,
        phrase_ref,
        second_out,
        first_out,
        phrase_out,
        first_weight,
        second_weight,
        encoded_grad,
        slope,
        second_grad,
        first_grad,
        first_sem,
        second_sem,
        row_sem,
    ) = refs[2 * planes + layout["arrays"] :]
    second_copies = load_weight(
        "second", layout, arrays, place_ref, chips, second_weight, second_sem
    )
    slope_copy = pltpu.make_async_copy(slope_ref, slope, row_sem.at[0])
    slope_copy.start()
    first_copies = load_weight("first", layout, arrays, place_ref, chips, first_weight, first_sem)
    join_halves(encoded_grad, place_ref[1], 0, mine, far)
    second_grad[...] = transposed_times(hidden_ref[...], encoded_grad[...])
    second_copy = pltpu.make_async_copy(second_grad, second_out, row_sem.at[1])
    second_copy.start()
    for copy in second_copies:
        copy.wait()
    hidden_grad = times_transposed(encoded_grad[...], second_weight[...])
    slope_copy.wait()
    act_grad = (hidden_grad * slope[...]).astype(jnp.bfloat16)
    first_grad[...] = transposed_times(phrase_ref[...], act_grad)
    first_copy = pltpu.make_async_copy(first_grad, first_out, row_sem.at[2])
    first_copy.start()
    for copy in first_copies:
        copy.wait()
    phrase_out[...] = times_transposed(
        act_grad[: phrase_out.shape[0]], first_weight[...]
    ).astype(jnp.bfloat16)
    second_copy.wait()
    first_copy.wait()


def attention_grads(
    latents,
    out_grad,
    query_weight,
    key_rows,
    value_rows,
    region_first,
    region_last,
    phrase_counts,
    offset,
):
    images, tokens, features = latents.shape
    slot_count = key_rows.shape[1]
    head_count = H
    head_size = features // head_count
    score_scale = head_size ** (-0.5)
    queries = jnp.dot(
        latents.reshape(images * tokens, features), query_weight, preferred_element_type=jnp.float32
    ).astype(jnp.bfloat16)
    query_heads = queries.reshape(images, tokens, head_count, head_size)
    key_heads = key_rows.reshape(images, slot_count, head_count, head_size)
    value_heads = value_rows.reshape(images, slot_count, head_count, head_size)
    grad_heads = out_grad.reshape(images, tokens, head_count, head_size)
    scores = (
        jnp.einsum("ithd,iphd->ithp", query_heads, key_heads, preferred_element_type=jnp.float32)
        * score_scale
    )
    block_ids = (offset + jnp.arange(tokens, dtype=jnp.int32)) // BLOCK
    phrase_ids = jnp.arange(slot_count, dtype=jnp.int32)
    visible = (
        (phrase_ids[None, None, :] < phrase_counts[:, None, None])
        & (region_first[:, None, :] <= block_ids[None, :, None])
        & (block_ids[None, :, None] <= region_last[:, None, :])
    )
    scores = jnp.where(visible[:, :, None, :], scores, -jnp.inf)
    row_max = jnp.max(scores, axis=-1, keepdims=True)
    exponent = jnp.exp(scores - row_max)
    attn_probs = exponent / jnp.sum(exponent, axis=-1, keepdims=True)
    probs_low = attn_probs.astype(jnp.bfloat16)
    prob_grad = jnp.einsum(
        "ithd,iphd->ithp", grad_heads, value_heads, preferred_element_type=jnp.float32
    )
    inner_sum = jnp.sum(attn_probs * prob_grad, axis=-1, keepdims=True)
    score_grad = (attn_probs * (prob_grad - inner_sum) * score_scale).astype(jnp.bfloat16)
    query_grad = jnp.einsum(
        "ithp,iphd->ithd", score_grad, key_heads, preferred_element_type=jnp.float32
    ).astype(jnp.bfloat16)
    latent_grad = times_transposed(
        query_grad.reshape(images * tokens, features), query_weight
    ).astype(jnp.bfloat16)
    key_part = jnp.einsum(
        "ithp,ithd->iphd", score_grad, query_heads, preferred_element_type=jnp.float32
    ).reshape(images, slot_count, features)
    value_part = jnp.einsum(
        "ithp,ithd->iphd", probs_low, grad_heads, preferred_element_type=jnp.float32
    ).reshape(images, slot_count, features)
    return (latent_grad.reshape(images, tokens, features), key_part, value_part)


def plain(
    latents,
    out_grad,
    phrases,
    query_weight,
    key_weight,
    value_weight,
    first_weight,
    second_weight,
    region_first,
    region_last,
    phrase_counts,
):
    images, tokens, features = latents.shape
    slot_count = phrases.shape[1]
    shard_rows = first_weight.shape[0]
    col_start = lax.axis_index("seq") * shard_rows
    phrase_rows = phrases.reshape(images * slot_count, features)

    def own_cols(matrix):
        return lax.dynamic_slice_in_dim(matrix, col_start, shard_rows, 1)

    full_first, full_second, full_key, full_value = (
        lax.all_gather(first_weight, "seq", axis=0, tiled=True),
        lax.all_gather(second_weight, "seq", axis=0, tiled=True),
        lax.all_gather(key_weight, "seq", axis=0, tiled=True),
        lax.all_gather(value_weight, "seq", axis=0, tiled=True),
    )
    pre_act = jnp.dot(phrase_rows, full_first, preferred_element_type=jnp.float32)
    hidden = jax.nn.silu(pre_act).astype(jnp.bfloat16)
    encoded = jnp.dot(hidden, full_second, preferred_element_type=jnp.float32).astype(jnp.bfloat16)
    key_rows = jnp.dot(encoded, full_key, preferred_element_type=jnp.float32).astype(jnp.bfloat16)
    value_rows = jnp.dot(encoded, full_value, preferred_element_type=jnp.float32).astype(
        jnp.bfloat16
    )
    offset = lax.axis_index("seq") * tokens
    latent_grad, key_part, value_part = attention_grads(
        latents,
        out_grad,
        query_weight,
        key_rows.reshape(images, slot_count, features),
        value_rows.reshape(images, slot_count, features),
        region_first,
        region_last,
        phrase_counts,
        offset,
    )
    key_sum_grad, value_sum_grad = lax.psum((key_part, value_part), "seq")
    key_grad = key_sum_grad.astype(jnp.bfloat16).reshape(images * slot_count, features)
    value_grad = value_sum_grad.astype(jnp.bfloat16).reshape(images * slot_count, features)
    encoded_grad = (
        times_transposed(key_grad, full_key) + times_transposed(value_grad, full_value)
    ).astype(jnp.bfloat16)
    second_grad = transposed_times(own_cols(hidden), encoded_grad)
    hidden_grad = times_transposed(encoded_grad, full_second)
    act_grad = (hidden_grad * silu_slope(pre_act)).astype(jnp.bfloat16)
    first_grad = transposed_times(own_cols(phrase_rows), act_grad)
    phrase_grad = times_transposed(act_grad, full_first).astype(jnp.bfloat16)
    first_grad, second_grad = lax.psum((first_grad, second_grad), "dp")
    return (latent_grad, phrase_grad.reshape(images, slot_count, features), first_grad, second_grad)


def local(shards, planes, *args):
    shard_rows = args[6].shape[0]
    if shard_rows % 16:
        return plain(*args)
    return tiled(shards, planes, *args)


def tiled(
    shards,
    planes,
    latents,
    out_grad,
    phrases,
    query_weight,
    key_weight,
    value_weight,
    first_weight,
    second_weight,
    region_first,
    region_last,
    phrase_counts,
):
    images, tokens, features = latents.shape
    slots = phrases.shape[1]
    shard_rows = first_weight.shape[0]
    chips = shards // 2
    rows = images * slots
    half = rows // 2
    shard, plane = lax.axis_index("seq"), lax.axis_index("dp")
    core = shard % 2
    place = jnp.stack([shard // 2, core, plane % 2]).astype(jnp.int32)
    shape = jax.ShapeDtypeStruct

    def swap(array, distance):
        return lax.ppermute(array, "seq", [(i, i ^ distance) for i in range(shards)])

    def swap_by_plane(array, even, odd):
        pairs = [
            (p * shards + i, p * shards + (i ^ (2 * (odd if p % 2 else even))))
            for p in range(planes)
            for i in range(shards)
        ]
        return lax.ppermute(array, ("dp", "seq"), pairs)

    def chip_peers(array):
        return [swap(array, 2 * k) for k in range(1, chips)]

    def plane_swap(array, distance):
        return lax.ppermute(array, "dp", [(i, i ^ distance) for i in range(planes)])

    def plane_peers(array):
        return [plane_swap(array, k) for k in range(1, planes)]

    def after(array, *others):
        return lax.optimization_barrier((array, *others))[0]

    def with_other_core(blocks):
        return blocks + [swap(block, 1) for block in blocks]

    def total_of(parts):
        return functools.reduce(jnp.add, [part.astype(jnp.float32) for part in parts])

    def project_queries(tokens_in):
        return jnp.dot(
            tokens_in.reshape(images * tokens, features),
            query_weight,
            preferred_element_type=jnp.float32,
        ).astype(jnp.bfloat16)

    phrase_rows = phrases.reshape(rows, features)
    bias = visible_bias(region_first, region_last, phrase_counts, shard * tokens, tokens)
    weight_shape = pltpu.VMEM((features, features), jnp.bfloat16)
    row_shape = pltpu.VMEM((images * tokens, features), jnp.bfloat16)
    sum_shape = pltpu.VMEM((rows, features), jnp.float32)
    block_sems = pltpu.SemaphoreType.DMA((2 * chips,))
    def join(parts, lengths, whole_rows):
        return pl.pallas_call(
            join_kernel,
            out_shape=[shape((whole_rows, features), jnp.bfloat16)] * lengths,
            in_specs=[VMEM] * len(parts),
            out_specs=[VMEM] * lengths,
            name="join",
        )(*parts)

    encoder, projector = join(
        [first_weight, second_weight, key_weight, value_weight], 2, 2 * shard_rows
    )
    if chips == 4:
        encoder_near = swap_by_plane(encoder, 1, 2)
        projector_near = swap_by_plane(projector, 2, 1)
        queries = project_queries(latents)
        encoder_own, projector_own = swap(encoder, 1), swap(projector, 1)
        own_half = lax.dynamic_slice_in_dim(
            after(phrase_rows, queries, encoder_own, projector_own, bias), core * half, half, 0
        )
        plane_phrases = plane_peers(own_half)
        encoder_next, projector_next, plane_phrases, value_next = lax.optimization_barrier(
            (encoder_near, projector_near, plane_phrases, value_weight)
        )
        encoder_far = swap_by_plane(encoder_next, 2, 1)
        encoder_third = plane_swap(encoder_next, 1)
        projector_far = swap_by_plane(projector_next, 1, 2)
        value_third = swap_by_plane(value_next, 1, 2)
        key_third = plane_swap(projector_next[:shard_rows], 1)
        far_phrases = [swap(part, 1) for part in plane_phrases]
        arrays = [encoder, encoder_near, projector, projector_near]
        arrays += [encoder_far, encoder_third, projector_far, key_third, value_third]
        swapped = [encoder_own, swap(encoder_next, 1), projector_own, swap(projector_next, 1)]
        encoder_far = after(encoder_far, *swapped, *far_phrases)
        arrays += swapped
        arrays += [
            swap(block, 1)
            for block in (encoder_far, encoder_third, projector_far, key_third, value_third)
        ]
        layout = {
            "first": (0, [(0, 0), (1, 0), (5, 0), (4, 0)]),
            "second": (0, [(i, shard_rows) for i in (0, 1, 5, 4)]),
            "key": (1, [(2, 0), (3, 0), (7, 0), (6, 0)]),
            "value": (1, [(2, shard_rows), (3, shard_rows), (8, 0), (6, shard_rows)]),
        }
    else:
        own_half = lax.dynamic_slice_in_dim(phrase_rows, core * half, half, 0)
        plane_phrases = plane_peers(own_half)
        far_phrases = [swap(part, 1) for part in plane_phrases]
        queries = project_queries(latents)
        arrays = [encoder] + chip_peers(encoder) + [projector] + chip_peers(projector)
        arrays += [swap(block, 1) for block in arrays]
        layout = {
            name: (0, [(first + k, offset) for k in range(chips)])
            for name, first, offset in (
                ("first", 0, 0),
                ("second", 0, shard_rows),
                ("key", chips, 0),
                ("value", chips, shard_rows),
            )
        }
    near_count = len(arrays) // 2
    for name, (scheme, blocks) in layout.items():
        layout[name] = (scheme, blocks + [(near_count + i, offset) for i, offset in blocks])
    layout["arrays"] = len(arrays)
    grads = out_grad.reshape(images * tokens, features)

    all_rows = planes * rows
    key_rows, score_grad, grad_mine, grad_other, slope, all_hidden, all_phrases = pl.pallas_call(
        functools.partial(attend_kernel, chips, planes, images, layout),
        out_shape=[
            shape((rows, features), jnp.bfloat16),
            shape((images, H * slots, tokens), jnp.bfloat16),
            shape((half, features), jnp.float32),
            shape((half, features), jnp.float32),
            shape((all_rows, features), jnp.float32),
            shape((all_rows, features), jnp.bfloat16),
            shape((all_rows, features), jnp.bfloat16),
        ],
        in_specs=[SMEM] + [VMEM] * (2 * planes - 1) + [HBM] * len(arrays) + [ANY] * 2 + [VMEM],
        out_specs=[VMEM, ANY, VMEM, VMEM, ANY, ANY, ANY],
        scratch_shapes=[
            weight_shape,
            weight_shape,
            weight_shape,
            weight_shape,
            row_shape,
            row_shape,
            pltpu.VMEM((all_rows, features), jnp.float32),
            pltpu.VMEM((all_rows, features), jnp.bfloat16),
            pltpu.VMEM((all_rows, features), jnp.bfloat16),
            pltpu.VMEM((images, H * slots, tokens), jnp.bfloat16),
            pltpu.VMEM((rows, features), jnp.bfloat16),
            sum_shape,
            sum_shape,
            sum_shape,
            block_sems,
            block_sems,
            block_sems,
            block_sems,
            pltpu.SemaphoreType.DMA((2,)),
            pltpu.SemaphoreType.DMA((3 + images,)),
        ],
        compiler_params=vmem(60),
        cost_estimate=pl.CostEstimate(
            flops=10**10, bytes_accessed=18 * 10**6, transcendentals=10**6
        ),
        name="attend",
    )(place, phrase_rows, *plane_phrases, *far_phrases, *arrays, queries, grads, bias)
    steps = 3 if features % 384 == 0 else 1
    tile = features // steps

    def latent_part(image, scores_in, whole=None):
        given = [] if whole is None else [whole]
        return pl.pallas_call(
            latent_kernel if whole is None else lambda _, *refs: latent_kernel(*refs),
            out_shape=shape((images * tokens, features), jnp.bfloat16),
            grid=(steps,),
            in_specs=[ANY] * len(given)
            + [
                pl.BlockSpec((1, H * slots, tokens), lambda t: (image, 0, 0)),
                pl.BlockSpec((slots, features), lambda t: (image, 0)),
                pl.BlockSpec((tile, features), lambda t: (t, 0)),
            ],
            out_specs=pl.BlockSpec((tokens, tile), lambda t: (image, t)),
            scratch_shapes=[pltpu.VMEM((tokens, features), jnp.bfloat16)],
            input_output_aliases={0: 0} if given else {},
            compiler_params=vmem(60),
            cost_estimate=pl.CostEstimate(
                flops=3 * 10**9, bytes_accessed=4 * 10**6, transcendentals=0
            ),
            name="latent",
        )(*given, scores_in, key_rows, query_weight)

    grad_pair = total_of([grad_mine, swap(grad_other, 1)]).astype(jnp.bfloat16)
    grad_own = total_of([grad_pair] + chip_peers(grad_pair)).astype(jnp.bfloat16)
    latent_grad = latent_part(0, score_grad)
    grad_own, latent_grad = lax.optimization_barrier((grad_own, latent_grad))
    own_hidden = lax.dynamic_slice_in_dim(all_hidden, shard * shard_rows, shard_rows, 1)
    all_own_phrases = lax.dynamic_slice_in_dim(all_phrases, shard * shard_rows, shard_rows, 1)
    for image in range(1, images):
        latent_grad = latent_part(image, score_grad, latent_grad)
    grad_mines = [grad_own] + plane_peers(grad_own)
    grad_fars = [swap(part, 1) for part in grad_mines]
    second_grad, first_grad, phrase_grad = pl.pallas_call(
        functools.partial(weight_grad_kernel, chips, planes, layout),
        out_shape=[
            shape((shard_rows, features), jnp.float32),
            shape((shard_rows, features), jnp.float32),
            shape((rows, features), jnp.bfloat16),
        ],
        in_specs=[SMEM] + [VMEM] * (2 * planes) + [ANY] * (len(arrays) + 1) + [VMEM] * 2,
        out_specs=[ANY, ANY, VMEM],
        scratch_shapes=[
            weight_shape,
            weight_shape,
            pltpu.VMEM((all_rows, features), jnp.bfloat16),
            pltpu.VMEM((all_rows, features), jnp.float32),
            pltpu.VMEM((shard_rows, features), jnp.float32),
            pltpu.VMEM((shard_rows, features), jnp.float32),
            block_sems,
            block_sems,
            pltpu.SemaphoreType.DMA((3,)),
        ],
        compiler_params=vmem(60),
        name="weight_grads",
    )(
        place,
        *grad_mines,
        *grad_fars,
        *arrays,
        slope,
        own_hidden,
        all_own_phrases,
    )
    return (
        latent_grad.reshape(images, tokens, features),
        phrase_grad.reshape(images, slots, features),
        first_grad,
        second_grad,
    )


def solution(mesh):
    shards, planes = mesh.shape["seq"], mesh.shape["dp"]
    in_specs = (
        P("dp", "seq", None),
        P("dp", "seq", None),
        P("dp", None, None),
        P(),
        P("seq", None),
        P("seq", None),
        P("seq", None),
        P("seq", None),
        P("dp", None),
        P("dp", None),
        P("dp"),
    )
    out_specs = (P("dp", "seq", None), P("dp", None, None), P("seq", None), P("seq", None))
    return jax.shard_map(
        functools.partial(local, shards, planes),
        mesh=mesh,
        in_specs=in_specs,
        out_specs=out_specs,
        check_vma=False,
    )
```

```python
import functools

import jax
import jax.numpy as jnp
from jax import lax
from jax.experimental import pallas as pl
from jax.experimental.pallas import tpu as pltpu
from jax.sharding import PartitionSpec as P

H = 16
BLOCK = 128
GROUP = 8
VMEM = pl.BlockSpec(memory_space=pltpu.VMEM)
SMEM = pl.BlockSpec(memory_space=pltpu.SMEM)
ANY = pl.BlockSpec(memory_space=pl.ANY)


def vmem(mebibytes):
    return pltpu.CompilerParams(vmem_limit_bytes=mebibytes * 1024 * 1024)


def silu_slope(pre_act):
    sigmoid = jax.nn.sigmoid(pre_act)
    return sigmoid * (1.0 + pre_act * (1.0 - sigmoid))


def contract(left_arg, right_arg, left_dim, right_dim):
    return lax.dot_general(
        left_arg,
        right_arg,
        (((left_dim,), (right_dim,)), ((), ())),
        preferred_element_type=jnp.float32,
    )


def times_transposed(left_arg, right_arg):
    return contract(left_arg, right_arg, 1, 1)


def transposed_times(left_arg, right_arg):
    return contract(left_arg, right_arg, 0, 0)


def split_times_transposed(left_arg, right_arg):
    rows = left_arg.shape[0]
    high = left_arg.astype(jnp.bfloat16)
    low = (left_arg - high.astype(jnp.float32)).astype(jnp.bfloat16)
    product = times_transposed(jnp.concatenate([high, low], axis=0), right_arg)
    return product[:rows] + product[rows:]


def visible_bias(region_first, region_last, phrase_counts, offset, tokens):
    block_ids = (offset + jnp.arange(tokens, dtype=jnp.int32)) // BLOCK
    phrase_ids = jnp.arange(region_first.shape[1], dtype=jnp.int32)
    visible = (
        (phrase_ids[None, :, None] < phrase_counts[:, None, None])
        & (region_first[:, :, None] <= block_ids[None, None, :])
        & (block_ids[None, None, :] <= region_last[:, :, None])
    )
    return jnp.where(visible, 0.0, -jnp.inf).astype(jnp.float32)


def window(group, head_size):
    start = group * GROUP * head_size
    return start // 128 * 128, -(-(start + GROUP * head_size) // 128) * 128


def own_columns(rows, group, head, head_size, low):
    first = (group * GROUP + head) * head_size - low
    column = lax.broadcasted_iota(jnp.int32, rows.shape, 1)
    return jnp.where((column >= first) & (column < first + head_size), rows, jnp.zeros_like(rows))


def block_diagonal(rows, group, head_size, low):
    return jnp.concatenate(
        [own_columns(rows, group, head, head_size, low) for head in range(GROUP)], axis=0
    )


def block_places(place_ref, scheme, chips):
    chip, core, odd = place_ref[0], place_ref[1], place_ref[2]
    steps = list(range(chips))
    if chips == 4:
        turn = odd if scheme == 0 else 1 - odd
        steps = [0, 1 + turn, 2 - turn, 3]
    return [2 * (chip ^ step) + other for other in (core, 1 - core) for step in steps]


def load_weight(name, layout, arrays, place_ref, chips, whole):
    scheme, blocks = layout[name]
    rows = whole.shape[0] // len(blocks)
    for (array, offset), place in zip(blocks, block_places(place_ref, scheme, chips)):
        whole[pl.ds(pl.multiple_of(place * rows, 16), rows)] = arrays[array][offset : offset + rows]


def project(left_arg, right_arg):
    return jnp.dot(left_arg, right_arg, preferred_element_type=jnp.float32)


def join_kernel(*refs):
    outs = [ref for ref in refs if ref.shape[0] == max(r.shape[0] for r in refs)]
    parts = iter(refs[: len(refs) - len(outs)])
    for out in outs:
        start = 0
        while start < out.shape[0]:
            part = next(parts)
            stop = min(start + part.shape[0], out.shape[0])
            out[start:stop] = part[: stop - start]
            start = stop


def join_halves(out_ref, core, start, mine, far):
    half = mine[0].shape[0]
    for plane in range(len(mine)):
        first = start + plane * 2 * half
        out_ref[pl.ds(pl.multiple_of(first + core * half, 16), half)] = mine[plane][...]
        out_ref[pl.ds(pl.multiple_of(first + (1 - core) * half, 16), half)] = far[plane][...]


def wait_all(copies):
    for copy in copies:
        copy.wait()


def encode_kernel(chips, planes, layout, place_ref, phrase_ref, *refs):
    others = planes - 1
    mine, far = refs[:others], refs[others : 2 * others]
    arrays = refs[2 * others : 2 * others + layout["arrays"]]
    (
        encoded_out,
        slope_out,
        own_hidden_out,
        own_phrase_out,
        first_weight,
        second_weight,
        phrases,
    ) = refs[2 * others + layout["arrays"] :]
    own_rows = phrase_ref.shape[0]
    phrases[:own_rows] = phrase_ref[...]
    join_halves(phrases, place_ref[1], own_rows, mine, far)
    load_weight("first", layout, arrays, place_ref, chips, first_weight)
    load_weight("second", layout, arrays, place_ref, chips, second_weight)
    columns = own_phrase_out.shape[1]
    selected = lax.broadcasted_iota(jnp.int32, (phrases.shape[1], columns), 0)
    selected -= (2 * place_ref[0] + place_ref[1]) * columns
    select = selected == lax.broadcasted_iota(jnp.int32, selected.shape, 1)
    select = jnp.where(select, 1.0, 0.0).astype(jnp.bfloat16)
    own_phrase_out[...] = project(phrases[...], select).astype(jnp.bfloat16)
    pre_act = project(phrases[...], first_weight[...])
    sigmoid = jax.nn.sigmoid(pre_act)
    hidden = (pre_act * sigmoid).astype(jnp.bfloat16)
    slope_out[...] = sigmoid * (1.0 + pre_act * (1.0 - sigmoid))
    own_hidden_out[...] = project(hidden, select).astype(jnp.bfloat16)
    encoded_out[...] = project(hidden[:own_rows], second_weight[...]).astype(jnp.bfloat16)


def head_parts(slots):
    return [slice(head * slots, (head + 1) * slots) for head in range(GROUP)]


def own_head_sum(full, group, head_size, low):
    slots = full.shape[0] // GROUP
    return functools.reduce(
        jnp.add,
        [
            own_columns(full[part], group, head, head_size, low)
            for head, part in enumerate(head_parts(slots))
        ],
    )


def attend_kernel(chips, images, layout, place_ref, encoded_ref, *refs):
    arrays = refs[: layout["arrays"]]
    (
        query,
        grad,
        bias_ref,
        key_out,
        score_out,
        mine_out,
        other_out,
        key_weight,
        value_weight,
        value_rows,
        key_sum,
        value_sum,
        total,
    ) = refs[layout["arrays"] :]
    own_rows = encoded_ref.shape[0]
    load_weight("key", layout, arrays, place_ref, chips, key_weight)
    load_weight("value", layout, arrays, place_ref, chips, value_weight)
    key_out[...] = project(encoded_ref[...], key_weight[...]).astype(jnp.bfloat16)
    value_rows[...] = project(encoded_ref[...], value_weight[...]).astype(jnp.bfloat16)

    slots = own_rows // images
    features = query.shape[1]
    tokens = query.shape[0] // images
    head_size = features // H
    scale = head_size ** (-0.5)
    key_sum[...] = jnp.zeros_like(key_sum)
    value_sum[...] = jnp.zeros_like(value_sum)
    for image in range(images):
        rows = pl.ds(image * slots, slots)
        here = pl.ds(image * tokens, tokens)
        bias = bias_ref[image]
        for group in range(H // GROUP):
            low, high = window(group, head_size)
            columns = pl.ds(low, high - low)
            keys = block_diagonal(key_out[rows, columns], group, head_size, low)
            values = block_diagonal(value_rows[rows, columns], group, head_size, low)
            queries = query[here, columns]
            grads = grad[here, columns]
            scores = times_transposed(keys, queries)
            prob_grad = times_transposed(values, grads)
            probs_low, score_grad = [], []
            for part in head_parts(slots):
                score = scores[part] * scale + bias
                exponent = jnp.exp(score - jnp.max(score, axis=0, keepdims=True))
                probs = exponent * (1.0 / jnp.sum(exponent, axis=0, keepdims=True))
                upstream = prob_grad[part]
                inner = jnp.sum(probs * upstream, axis=0, keepdims=True)
                probs_low.append(probs.astype(jnp.bfloat16))
                score_grad.append((probs * (upstream - inner) * scale).astype(jnp.bfloat16))
            probs_low = jnp.concatenate(probs_low, axis=0)
            score_grad = jnp.concatenate(score_grad, axis=0)
            score_out[image, pl.ds(group * GROUP * slots, GROUP * slots)] = score_grad
            key_sum[rows, columns] += own_head_sum(
                project(score_grad, queries), group, head_size, low
            )
            value_sum[rows, columns] += own_head_sum(
                project(probs_low, grads), group, head_size, low
            )
    total[...] = split_times_transposed(key_sum[...], key_weight[...]) + split_times_transposed(
        value_sum[...], value_weight[...]
    )
    core = place_ref[1]
    half = mine_out.shape[0]
    mine_out[...] = total[pl.ds(pl.multiple_of(core * half, 8), half)]
    other_out[...] = total[pl.ds(pl.multiple_of((1 - core) * half, 8), half)]


def latent_kernel(image, score_ref, key_ref, weight, out_ref, result, out_sem):
    slots, features = key_ref.shape[0] // score_ref.shape[0], weight.shape[0]
    tokens = score_ref.shape[2]
    head_size = features // H
    parts = []
    for group in range(H // GROUP):
        low, high = window(group, head_size)
        rows = key_ref[image * slots : (image + 1) * slots, low:high]
        keys = block_diagonal(rows, group, head_size, low)
        score_grad = score_ref[image, group * GROUP * slots : (group + 1) * GROUP * slots]
        part = transposed_times(score_grad, keys)
        if low:
            part = jnp.concatenate([jnp.zeros((part.shape[0], low), jnp.float32), part], axis=1)
        if high < features:
            part = jnp.concatenate(
                [part, jnp.zeros((part.shape[0], features - high), jnp.float32)], axis=1
            )
        parts.append(part)
    query_grad = functools.reduce(jnp.add, parts).astype(jnp.bfloat16)
    tile = tokens // out_sem.shape[0]
    copies = []
    for step in range(out_sem.shape[0]):
        rows = slice(step * tile, (step + 1) * tile)
        result[rows] = times_transposed(query_grad[rows], weight[...]).astype(jnp.bfloat16)
        copies.append(
            pltpu.make_async_copy(
                result.at[rows], out_ref.at[pl.ds(image * tokens + step * tile, tile)], out_sem.at[step]
            )
        )
        copies[-1].start()
    wait_all(copies)


def weight_grad_kernel(planes, place_ref, *refs):
    mine, far = refs[:planes], refs[planes : 2 * planes]
    (
        first_weight,
        second_weight,
        slope_ref,
        hidden_ref,
        phrase_ref,
        second_out,
        first_out,
        phrase_out,
        encoded_grad,
        second_grad,
        first_grad,
        out_sem,
    ) = refs[2 * planes :]
    join_halves(encoded_grad, place_ref[1], 0, mine, far)
    second_grad[...] = transposed_times(hidden_ref[...], encoded_grad[...])
    second_copy = pltpu.make_async_copy(second_grad, second_out, out_sem.at[0])
    second_copy.start()
    hidden_grad = times_transposed(encoded_grad[...], second_weight[...])
    act_grad = (hidden_grad * slope_ref[...]).astype(jnp.bfloat16)
    first_grad[...] = transposed_times(phrase_ref[...], act_grad)
    first_copy = pltpu.make_async_copy(first_grad, first_out, out_sem.at[1])
    first_copy.start()
    phrase_out[...] = times_transposed(
        act_grad[: phrase_out.shape[0]], first_weight[...]
    ).astype(jnp.bfloat16)
    second_copy.wait()
    first_copy.wait()


def attention_grads(
    latents,
    out_grad,
    query_weight,
    key_rows,
    value_rows,
    region_first,
    region_last,
    phrase_counts,
    offset,
):
    images, tokens, features = latents.shape
    slot_count = key_rows.shape[1]
    head_count = H
    head_size = features // head_count
    score_scale = head_size ** (-0.5)
    queries = jnp.dot(
        latents.reshape(images * tokens, features), query_weight, preferred_element_type=jnp.float32
    ).astype(jnp.bfloat16)
    query_heads = queries.reshape(images, tokens, head_count, head_size)
    key_heads = key_rows.reshape(images, slot_count, head_count, head_size)
    value_heads = value_rows.reshape(images, slot_count, head_count, head_size)
    grad_heads = out_grad.reshape(images, tokens, head_count, head_size)
    scores = (
        jnp.einsum("ithd,iphd->ithp", query_heads, key_heads, preferred_element_type=jnp.float32)
        * score_scale
    )
    block_ids = (offset + jnp.arange(tokens, dtype=jnp.int32)) // BLOCK
    phrase_ids = jnp.arange(slot_count, dtype=jnp.int32)
    visible = (
        (phrase_ids[None, None, :] < phrase_counts[:, None, None])
        & (region_first[:, None, :] <= block_ids[None, :, None])
        & (block_ids[None, :, None] <= region_last[:, None, :])
    )
    scores = jnp.where(visible[:, :, None, :], scores, -jnp.inf)
    row_max = jnp.max(scores, axis=-1, keepdims=True)
    exponent = jnp.exp(scores - row_max)
    attn_probs = exponent / jnp.sum(exponent, axis=-1, keepdims=True)
    probs_low = attn_probs.astype(jnp.bfloat16)
    prob_grad = jnp.einsum(
        "ithd,iphd->ithp", grad_heads, value_heads, preferred_element_type=jnp.float32
    )
    inner_sum = jnp.sum(attn_probs * prob_grad, axis=-1, keepdims=True)
    score_grad = (attn_probs * (prob_grad - inner_sum) * score_scale).astype(jnp.bfloat16)
    query_grad = jnp.einsum(
        "ithp,iphd->ithd", score_grad, key_heads, preferred_element_type=jnp.float32
    ).astype(jnp.bfloat16)
    latent_grad = times_transposed(
        query_grad.reshape(images * tokens, features), query_weight
    ).astype(jnp.bfloat16)
    key_part = jnp.einsum(
        "ithp,ithd->iphd", score_grad, query_heads, preferred_element_type=jnp.float32
    ).reshape(images, slot_count, features)
    value_part = jnp.einsum(
        "ithp,ithd->iphd", probs_low, grad_heads, preferred_element_type=jnp.float32
    ).reshape(images, slot_count, features)
    return (latent_grad.reshape(images, tokens, features), key_part, value_part)


def plain(
    latents,
    out_grad,
    phrases,
    query_weight,
    key_weight,
    value_weight,
    first_weight,
    second_weight,
    region_first,
    region_last,
    phrase_counts,
):
    images, tokens, features = latents.shape
    slot_count = phrases.shape[1]
    shard_rows = first_weight.shape[0]
    col_start = lax.axis_index("seq") * shard_rows
    phrase_rows = phrases.reshape(images * slot_count, features)

    def own_cols(matrix):
        return lax.dynamic_slice_in_dim(matrix, col_start, shard_rows, 1)

    full_first, full_second, full_key, full_value = (
        lax.all_gather(first_weight, "seq", axis=0, tiled=True),
        lax.all_gather(second_weight, "seq", axis=0, tiled=True),
        lax.all_gather(key_weight, "seq", axis=0, tiled=True),
        lax.all_gather(value_weight, "seq", axis=0, tiled=True),
    )
    pre_act = jnp.dot(phrase_rows, full_first, preferred_element_type=jnp.float32)
    hidden = jax.nn.silu(pre_act).astype(jnp.bfloat16)
    encoded = jnp.dot(hidden, full_second, preferred_element_type=jnp.float32).astype(jnp.bfloat16)
    key_rows = jnp.dot(encoded, full_key, preferred_element_type=jnp.float32).astype(jnp.bfloat16)
    value_rows = jnp.dot(encoded, full_value, preferred_element_type=jnp.float32).astype(
        jnp.bfloat16
    )
    offset = lax.axis_index("seq") * tokens
    latent_grad, key_part, value_part = attention_grads(
        latents,
        out_grad,
        query_weight,
        key_rows.reshape(images, slot_count, features),
        value_rows.reshape(images, slot_count, features),
        region_first,
        region_last,
        phrase_counts,
        offset,
    )
    key_sum_grad, value_sum_grad = lax.psum((key_part, value_part), "seq")
    key_grad = key_sum_grad.astype(jnp.bfloat16).reshape(images * slot_count, features)
    value_grad = value_sum_grad.astype(jnp.bfloat16).reshape(images * slot_count, features)
    encoded_grad = (
        times_transposed(key_grad, full_key) + times_transposed(value_grad, full_value)
    ).astype(jnp.bfloat16)
    second_grad = transposed_times(own_cols(hidden), encoded_grad)
    hidden_grad = times_transposed(encoded_grad, full_second)
    act_grad = (hidden_grad * silu_slope(pre_act)).astype(jnp.bfloat16)
    first_grad = transposed_times(own_cols(phrase_rows), act_grad)
    phrase_grad = times_transposed(act_grad, full_first).astype(jnp.bfloat16)
    first_grad, second_grad = lax.psum((first_grad, second_grad), "dp")
    return (latent_grad, phrase_grad.reshape(images, slot_count, features), first_grad, second_grad)


def local(shards, planes, *args):
    shard_rows = args[6].shape[0]
    if shard_rows % 16:
        return plain(*args)
    return tiled(shards, planes, *args)


def tiled(
    shards,
    planes,
    latents,
    out_grad,
    phrases,
    query_weight,
    key_weight,
    value_weight,
    first_weight,
    second_weight,
    region_first,
    region_last,
    phrase_counts,
):
    images, tokens, features = latents.shape
    slots = phrases.shape[1]
    shard_rows = first_weight.shape[0]
    chips = shards // 2
    rows = images * slots
    half = rows // 2
    shard, plane = lax.axis_index("seq"), lax.axis_index("dp")
    core = shard % 2
    place = jnp.stack([shard // 2, core, plane % 2]).astype(jnp.int32)
    shape = jax.ShapeDtypeStruct

    def swap(array, distance):
        return lax.ppermute(array, "seq", [(i, i ^ distance) for i in range(shards)])

    def swap_by_plane(array, even, odd):
        pairs = [
            (p * shards + i, p * shards + (i ^ (2 * (odd if p % 2 else even))))
            for p in range(planes)
            for i in range(shards)
        ]
        return lax.ppermute(array, ("dp", "seq"), pairs)

    def chip_peers(array):
        return [swap(array, 2 * k) for k in range(1, chips)]

    def plane_swap(array, distance):
        return lax.ppermute(array, "dp", [(i, i ^ distance) for i in range(planes)])

    def plane_peers(array):
        return [plane_swap(array, k) for k in range(1, planes)]

    def after_all(parts, *others):
        return lax.optimization_barrier((*parts, *others))[: len(parts)]

    def after(array, *others):
        return lax.optimization_barrier((array, *others))[0]

    def with_other_core(blocks):
        return blocks + [swap(block, 1) for block in blocks]

    def total_of(parts):
        return functools.reduce(jnp.add, [part.astype(jnp.float32) for part in parts])

    def project_queries(tokens_in):
        return jnp.dot(
            tokens_in.reshape(images * tokens, features),
            query_weight,
            preferred_element_type=jnp.float32,
        ).astype(jnp.bfloat16)

    phrase_rows = phrases.reshape(rows, features)
    bias = visible_bias(region_first, region_last, phrase_counts, shard * tokens, tokens)
    weight_shape = pltpu.VMEM((features, features), jnp.bfloat16)
    sum_shape = pltpu.VMEM((rows, features), jnp.float32)
    def join(parts, lengths, whole_rows):
        return pl.pallas_call(
            join_kernel,
            out_shape=[shape((whole_rows, features), jnp.bfloat16)] * lengths,
            in_specs=[VMEM] * len(parts),
            out_specs=[VMEM] * lengths,
            name="join",
        )(*parts)

    encoder, projector = join(
        [first_weight, second_weight, key_weight, value_weight], 2, 2 * shard_rows
    )
    if chips == 4:
        encoder_near = swap_by_plane(encoder, 1, 2)
        projector_near = swap_by_plane(projector, 2, 1)
        encoder_own, projector_own = swap(encoder, 1), swap(projector, 1)
        own_half = lax.dynamic_slice_in_dim(
            after(phrase_rows, encoder_own, projector_own), core * half, half, 0
        )
        queries = project_queries(after(latents, encoder_own, projector_own))
        plane_phrases = plane_peers(own_half)
        far_phrases = [swap(part, 1) for part in after_all(plane_phrases, queries)]
        encoder_next, projector_next, value_next, far_phrases, queries, bias, place = (
            lax.optimization_barrier(
                (encoder_near, projector_near, value_weight, far_phrases, queries, bias, place)
            )
        )
        value_third = swap_by_plane(value_next, 1, 2)
        encoder_far = swap_by_plane(encoder_next, 2, 1)
        encoder_third = plane_swap(encoder_next, 1)
        pairs = [swap(encoder_next, 1), swap(projector_next, 1)]
        projector_next = after(projector_next, *pairs)
        projector_far = swap_by_plane(projector_next, 1, 2)
        key_third = plane_swap(projector_next[:shard_rows], 1)
        arrays = [encoder, encoder_near, projector, projector_near]
        arrays += [encoder_far, encoder_third, projector_far, key_third, value_third]
        arrays += [encoder_own, pairs[0], projector_own, pairs[1]]
        arrays += [swap(block, 1) for block in arrays[4:9]]
        arrays = list(lax.optimization_barrier(tuple(arrays)))
        layout = {
            "first": (0, [(0, 0), (1, 0), (5, 0), (4, 0)]),
            "second": (0, [(i, shard_rows) for i in (0, 1, 5, 4)]),
            "key": (1, [(2, 0), (3, 0), (7, 0), (6, 0)]),
            "value": (1, [(2, shard_rows), (3, shard_rows), (8, 0), (6, shard_rows)]),
        }
    else:
        own_half = lax.dynamic_slice_in_dim(phrase_rows, core * half, half, 0)
        plane_phrases = plane_peers(own_half)
        far_phrases = [swap(part, 1) for part in plane_phrases]
        queries = project_queries(latents)
        arrays = [encoder] + chip_peers(encoder) + [projector] + chip_peers(projector)
        arrays += [swap(block, 1) for block in arrays]
        layout = {
            name: (0, [(first + k, offset) for k in range(chips)])
            for name, first, offset in (
                ("first", 0, 0),
                ("second", 0, shard_rows),
                ("key", chips, 0),
                ("value", chips, shard_rows),
            )
        }
    near_count = chips == 4 and 9 or len(arrays) // 2
    for name, (scheme, blocks) in layout.items():
        layout[name] = (scheme, blocks + [(near_count + i, offset) for i, offset in blocks])

    def weights(*names):
        used = sorted({i for name in names for i, _ in layout[name][1]})
        own_layout = {
            name: (layout[name][0], [(used.index(i), offset) for i, offset in layout[name][1]])
            for name in names
        }
        return [arrays[i] for i in used], {**own_layout, "arrays": len(used)}

    all_rows = planes * rows
    encoder_arrays, encoder_layout = weights("first", "second")
    encoded, slope, own_hidden, own_phrases, whole_first, whole_second = pl.pallas_call(
        functools.partial(encode_kernel, chips, planes, encoder_layout),
        out_shape=[
            shape((rows, features), jnp.bfloat16),
            shape((all_rows, features), jnp.float32),
            shape((all_rows, shard_rows), jnp.bfloat16),
            shape((all_rows, shard_rows), jnp.bfloat16),
            shape((features, features), jnp.bfloat16),
            shape((features, features), jnp.bfloat16),
        ],
        in_specs=[SMEM] + [VMEM] * (2 * planes - 1 + len(encoder_arrays)),
        out_specs=[VMEM] * 6,
        scratch_shapes=[pltpu.VMEM((all_rows, features), jnp.bfloat16)],
        compiler_params=vmem(18),
        cost_estimate=pl.CostEstimate(
            flops=2 * 10**9, bytes_accessed=8 * 10**6, transcendentals=10**5
        ),
        name="encode",
    )(place, phrase_rows, *plane_phrases, *far_phrases, *encoder_arrays)
    grads = out_grad.reshape(images * tokens, features)
    projector_arrays, projector_layout = weights("key", "value")
    key_rows, score_grad, grad_mine, grad_other = pl.pallas_call(
        functools.partial(attend_kernel, chips, images, projector_layout),
        out_shape=[
            shape((rows, features), jnp.bfloat16),
            shape((images, H * slots, tokens), jnp.bfloat16),
            shape((half, features), jnp.float32),
            shape((half, features), jnp.float32),
        ],
        in_specs=[SMEM] + [VMEM] * (len(projector_arrays) + 4),
        out_specs=[VMEM] * 4,
        scratch_shapes=[
            weight_shape,
            weight_shape,
            pltpu.VMEM((rows, features), jnp.bfloat16),
            sum_shape,
            sum_shape,
            sum_shape,
        ],
        compiler_params=vmem(28),
        cost_estimate=pl.CostEstimate(
            flops=10**10, bytes_accessed=12 * 10**6, transcendentals=10**6
        ),
        name="attend",
    )(place, encoded, *projector_arrays, queries, grads, bias)

    def latent_part(image, scores_in, whole=None):
        given = [] if whole is None else [whole]
        kernel = functools.partial(latent_kernel, image)
        return pl.pallas_call(
            kernel if whole is None else lambda _, *refs: kernel(*refs),
            out_shape=shape((images * tokens, features), jnp.bfloat16),
            in_specs=[ANY] * len(given) + [VMEM] * 3,
            out_specs=ANY,
            scratch_shapes=[
                pltpu.VMEM((tokens, features), jnp.bfloat16),
                pltpu.SemaphoreType.DMA((2,)),
            ],
            input_output_aliases={0: 0} if given else {},
            compiler_params=vmem(12),
            cost_estimate=pl.CostEstimate(
                flops=3 * 10**9, bytes_accessed=4 * 10**6, transcendentals=0
            ),
            name="latent",
        )(*given, scores_in, key_rows, query_weight)

    grad_pair = total_of([grad_mine, swap(grad_other, 1)]).astype(jnp.bfloat16)
    grad_own = total_of([grad_pair] + chip_peers(grad_pair)).astype(jnp.bfloat16)
    latent_grad = latent_part(0, score_grad)
    grad_own, latent_grad = lax.optimization_barrier((grad_own, latent_grad))
    for image in range(1, images):
        latent_grad = latent_part(image, score_grad, latent_grad)
    grad_mines = [grad_own] + plane_peers(grad_own)
    grad_fars = [swap(grad_own, 1)]
    grad_fars += [swap(part, 1) for part in after_all(grad_mines[1:], latent_grad)]
    second_grad, first_grad, phrase_grad = pl.pallas_call(
        functools.partial(weight_grad_kernel, planes),
        out_shape=[
            shape((shard_rows, features), jnp.float32),
            shape((shard_rows, features), jnp.float32),
            shape((rows, features), jnp.bfloat16),
        ],
        in_specs=[SMEM] + [VMEM] * (2 * planes + 5),
        out_specs=[ANY, ANY, VMEM],
        scratch_shapes=[
            pltpu.VMEM((all_rows, features), jnp.bfloat16),
            pltpu.VMEM((shard_rows, features), jnp.float32),
            pltpu.VMEM((shard_rows, features), jnp.float32),
            pltpu.SemaphoreType.DMA((2,)),
        ],
        compiler_params=vmem(20),
        name="weight_grads",
    )(
        place,
        *grad_mines,
        *grad_fars,
        whole_first,
        whole_second,
        slope,
        own_hidden,
        own_phrases,
    )
    return (
        latent_grad.reshape(images, tokens, features),
        phrase_grad.reshape(images, slots, features),
        first_grad,
        second_grad,
    )


def solution(mesh):
    shards, planes = mesh.shape["seq"], mesh.shape["dp"]
    in_specs = (
        P("dp", "seq", None),
        P("dp", "seq", None),
        P("dp", None, None),
        P(),
        P("seq", None),
        P("seq", None),
        P("seq", None),
        P("seq", None),
        P("dp", None),
        P("dp", None),
        P("dp"),
    )
    out_specs = (P("dp", "seq", None), P("dp", None, None), P("seq", None), P("seq", None))
    return jax.shard_map(
        functools.partial(local, shards, planes),
        mesh=mesh,
        in_specs=in_specs,
        out_specs=out_specs,
        check_vma=False,
    )
```

```python
import functools

import jax
import jax.numpy as jnp
from jax import lax
from jax.experimental import pallas as pl
from jax.experimental.pallas import tpu as pltpu
from jax.sharding import PartitionSpec as P

H = 16
BLOCK = 128
GROUP = 8
VMEM = pl.BlockSpec(memory_space=pltpu.VMEM)
SMEM = pl.BlockSpec(memory_space=pltpu.SMEM)
ANY = pl.BlockSpec(memory_space=pl.ANY)


def vmem(mebibytes):
    return pltpu.CompilerParams(vmem_limit_bytes=mebibytes * 1024 * 1024)


def silu_slope(pre_act):
    sigmoid = jax.nn.sigmoid(pre_act)
    return sigmoid * (1.0 + pre_act * (1.0 - sigmoid))


def contract(left_arg, right_arg, left_dim, right_dim):
    return lax.dot_general(
        left_arg,
        right_arg,
        (((left_dim,), (right_dim,)), ((), ())),
        preferred_element_type=jnp.float32,
    )


def times_transposed(left_arg, right_arg):
    return contract(left_arg, right_arg, 1, 1)


def transposed_times(left_arg, right_arg):
    return contract(left_arg, right_arg, 0, 0)


def split_times_transposed(left_arg, right_arg):
    rows = left_arg.shape[0]
    high = left_arg.astype(jnp.bfloat16)
    low = (left_arg - high.astype(jnp.float32)).astype(jnp.bfloat16)
    product = times_transposed(jnp.concatenate([high, low], axis=0), right_arg)
    return product[:rows] + product[rows:]


def visible_bias(region_first, region_last, phrase_counts, offset, tokens):
    block_ids = (offset + jnp.arange(tokens, dtype=jnp.int32)) // BLOCK
    phrase_ids = jnp.arange(region_first.shape[1], dtype=jnp.int32)
    visible = (
        (phrase_ids[None, :, None] < phrase_counts[:, None, None])
        & (region_first[:, :, None] <= block_ids[None, None, :])
        & (block_ids[None, None, :] <= region_last[:, :, None])
    )
    return jnp.where(visible, 0.0, -jnp.inf).astype(jnp.float32)


def window(group, head_size):
    start = group * GROUP * head_size
    return start // 128 * 128, -(-(start + GROUP * head_size) // 128) * 128


def own_columns(rows, group, head, head_size, low):
    first = (group * GROUP + head) * head_size - low
    column = lax.broadcasted_iota(jnp.int32, rows.shape, 1)
    return jnp.where((column >= first) & (column < first + head_size), rows, jnp.zeros_like(rows))


def block_diagonal(rows, group, head_size, low):
    return jnp.concatenate(
        [own_columns(rows, group, head, head_size, low) for head in range(GROUP)], axis=0
    )


def block_places(place_ref, scheme, chips):
    chip, core, odd = place_ref[0], place_ref[1], place_ref[2]
    steps = list(range(chips))
    if chips == 4:
        turn = odd if scheme == 0 else 1 - odd
        steps = [0, 1 + turn, 2 - turn, 3]
    return [2 * (chip ^ step) + other for other in (core, 1 - core) for step in steps]


def load_weight(name, layout, arrays, place_ref, chips, whole):
    scheme, blocks = layout[name]
    rows = whole.shape[0] // len(blocks)
    for (array, offset), place in zip(blocks, block_places(place_ref, scheme, chips)):
        whole[pl.ds(pl.multiple_of(place * rows, 16), rows)] = arrays[array][offset : offset + rows]


def project(left_arg, right_arg):
    return jnp.dot(left_arg, right_arg, preferred_element_type=jnp.float32)


def join_kernel(*refs):
    outs = [ref for ref in refs if ref.shape[0] == max(r.shape[0] for r in refs)]
    parts = iter(refs[: len(refs) - len(outs)])
    for out in outs:
        start = 0
        while start < out.shape[0]:
            part = next(parts)
            stop = min(start + part.shape[0], out.shape[0])
            out[start:stop] = part[: stop - start]
            start = stop


def join_halves(out_ref, core, start, mine, far):
    half = mine[0].shape[0]
    for plane in range(len(mine)):
        first = start + plane * 2 * half
        out_ref[pl.ds(pl.multiple_of(first + core * half, 16), half)] = mine[plane][...]
        out_ref[pl.ds(pl.multiple_of(first + (1 - core) * half, 16), half)] = far[plane][...]


def wait_all(copies):
    for copy in copies:
        copy.wait()


def encode_kernel(chips, planes, layout, place_ref, phrase_ref, *refs):
    others = planes - 1
    mine, far = refs[:others], refs[others : 2 * others]
    arrays = refs[2 * others : 2 * others + layout["arrays"]]
    (
        encoded_out,
        slope_out,
        own_hidden_out,
        own_phrase_out,
        first_weight,
        second_weight,
        phrases,
    ) = refs[2 * others + layout["arrays"] :]
    own_rows = phrase_ref.shape[0]
    phrases[:own_rows] = phrase_ref[...]
    join_halves(phrases, place_ref[1], own_rows, mine, far)
    load_weight("first", layout, arrays, place_ref, chips, first_weight)
    load_weight("second", layout, arrays, place_ref, chips, second_weight)
    columns = own_phrase_out.shape[1]
    selected = lax.broadcasted_iota(jnp.int32, (phrases.shape[1], columns), 0)
    selected -= (2 * place_ref[0] + place_ref[1]) * columns
    select = selected == lax.broadcasted_iota(jnp.int32, selected.shape, 1)
    select = jnp.where(select, 1.0, 0.0).astype(jnp.bfloat16)
    own_phrase_out[...] = project(phrases[...], select).astype(jnp.bfloat16)
    pre_act = project(phrases[...], first_weight[...])
    sigmoid = jax.nn.sigmoid(pre_act)
    hidden = (pre_act * sigmoid).astype(jnp.bfloat16)
    slope_out[...] = sigmoid * (1.0 + pre_act * (1.0 - sigmoid))
    own_hidden_out[...] = project(hidden, select).astype(jnp.bfloat16)
    encoded_out[...] = project(hidden[:own_rows], second_weight[...]).astype(jnp.bfloat16)


def head_parts(slots):
    return [slice(head * slots, (head + 1) * slots) for head in range(GROUP)]


def own_head_sum(full, group, head_size, low):
    slots = full.shape[0] // GROUP
    return functools.reduce(
        jnp.add,
        [
            own_columns(full[part], group, head, head_size, low)
            for head, part in enumerate(head_parts(slots))
        ],
    )


def attend_kernel(chips, images, layout, place_ref, encoded_ref, *refs):
    arrays = refs[: layout["arrays"]]
    (
        query,
        grad,
        bias_ref,
        key_out,
        score_out,
        mine_out,
        other_out,
        key_weight,
        value_weight,
        value_rows,
        key_sum,
        value_sum,
        total,
    ) = refs[layout["arrays"] :]
    own_rows = encoded_ref.shape[0]
    load_weight("key", layout, arrays, place_ref, chips, key_weight)
    load_weight("value", layout, arrays, place_ref, chips, value_weight)
    key_out[...] = project(encoded_ref[...], key_weight[...]).astype(jnp.bfloat16)
    value_rows[...] = project(encoded_ref[...], value_weight[...]).astype(jnp.bfloat16)

    slots = own_rows // images
    features = query.shape[1]
    tokens = query.shape[0] // images
    head_size = features // H
    scale = head_size ** (-0.5)
    key_sum[...] = jnp.zeros_like(key_sum)
    value_sum[...] = jnp.zeros_like(value_sum)
    for image in range(images):
        rows = pl.ds(image * slots, slots)
        here = pl.ds(image * tokens, tokens)
        bias = bias_ref[image]
        for group in range(H // GROUP):
            low, high = window(group, head_size)
            columns = pl.ds(low, high - low)
            keys = block_diagonal(key_out[rows, columns], group, head_size, low)
            values = block_diagonal(value_rows[rows, columns], group, head_size, low)
            queries = query[here, columns]
            grads = grad[here, columns]
            scores = times_transposed(keys, queries)
            prob_grad = times_transposed(values, grads)
            probs_low, score_grad = [], []
            for part in head_parts(slots):
                score = scores[part] * scale + bias
                exponent = jnp.exp(score - jnp.max(score, axis=0, keepdims=True))
                probs = exponent * (1.0 / jnp.sum(exponent, axis=0, keepdims=True))
                upstream = prob_grad[part]
                inner = jnp.sum(probs * upstream, axis=0, keepdims=True)
                probs_low.append(probs.astype(jnp.bfloat16))
                score_grad.append((probs * (upstream - inner) * scale).astype(jnp.bfloat16))
            probs_low = jnp.concatenate(probs_low, axis=0)
            score_grad = jnp.concatenate(score_grad, axis=0)
            score_out[image, pl.ds(group * GROUP * slots, GROUP * slots)] = score_grad
            key_sum[rows, columns] += own_head_sum(
                project(score_grad, queries), group, head_size, low
            )
            value_sum[rows, columns] += own_head_sum(
                project(probs_low, grads), group, head_size, low
            )
    total[...] = split_times_transposed(key_sum[...], key_weight[...]) + split_times_transposed(
        value_sum[...], value_weight[...]
    )
    core = place_ref[1]
    half = mine_out.shape[0]
    mine_out[...] = total[pl.ds(pl.multiple_of(core * half, 8), half)]
    other_out[...] = total[pl.ds(pl.multiple_of((1 - core) * half, 8), half)]


def latent_kernel(image, score_ref, key_ref, weight, out_ref, result, out_sem):
    slots, features = key_ref.shape[0] // score_ref.shape[0], weight.shape[0]
    tokens = score_ref.shape[2]
    head_size = features // H
    parts = []
    for group in range(H // GROUP):
        low, high = window(group, head_size)
        rows = key_ref[image * slots : (image + 1) * slots, low:high]
        keys = block_diagonal(rows, group, head_size, low)
        score_grad = score_ref[image, group * GROUP * slots : (group + 1) * GROUP * slots]
        part = transposed_times(score_grad, keys)
        if low:
            part = jnp.concatenate([jnp.zeros((part.shape[0], low), jnp.float32), part], axis=1)
        if high < features:
            part = jnp.concatenate(
                [part, jnp.zeros((part.shape[0], features - high), jnp.float32)], axis=1
            )
        parts.append(part)
    query_grad = functools.reduce(jnp.add, parts).astype(jnp.bfloat16)
    tile = tokens // out_sem.shape[0]
    copies = []
    for step in range(out_sem.shape[0]):
        rows = slice(step * tile, (step + 1) * tile)
        result[rows] = times_transposed(query_grad[rows], weight[...]).astype(jnp.bfloat16)
        copies.append(
            pltpu.make_async_copy(
                result.at[rows], out_ref.at[pl.ds(image * tokens + step * tile, tile)], out_sem.at[step]
            )
        )
        copies[-1].start()
    wait_all(copies)


def weight_grad_kernel(planes, place_ref, *refs):
    mine, far = refs[:planes], refs[planes : 2 * planes]
    (
        first_weight,
        second_weight,
        slope_ref,
        hidden_ref,
        phrase_ref,
        second_out,
        first_out,
        phrase_out,
        encoded_grad,
        second_grad,
        first_grad,
        out_sem,
    ) = refs[2 * planes :]
    join_halves(encoded_grad, place_ref[1], 0, mine, far)
    second_grad[...] = transposed_times(hidden_ref[...], encoded_grad[...])
    second_copy = pltpu.make_async_copy(second_grad, second_out, out_sem.at[0])
    second_copy.start()
    hidden_grad = times_transposed(encoded_grad[...], second_weight[...])
    act_grad = (hidden_grad * slope_ref[...]).astype(jnp.bfloat16)
    first_grad[...] = transposed_times(phrase_ref[...], act_grad)
    first_copy = pltpu.make_async_copy(first_grad, first_out, out_sem.at[1])
    first_copy.start()
    phrase_out[...] = times_transposed(
        act_grad[: phrase_out.shape[0]], first_weight[...]
    ).astype(jnp.bfloat16)
    second_copy.wait()
    first_copy.wait()


def attention_grads(
    latents,
    out_grad,
    query_weight,
    key_rows,
    value_rows,
    region_first,
    region_last,
    phrase_counts,
    offset,
):
    images, tokens, features = latents.shape
    slot_count = key_rows.shape[1]
    head_count = H
    head_size = features // head_count
    score_scale = head_size ** (-0.5)
    queries = jnp.dot(
        latents.reshape(images * tokens, features), query_weight, preferred_element_type=jnp.float32
    ).astype(jnp.bfloat16)
    query_heads = queries.reshape(images, tokens, head_count, head_size)
    key_heads = key_rows.reshape(images, slot_count, head_count, head_size)
    value_heads = value_rows.reshape(images, slot_count, head_count, head_size)
    grad_heads = out_grad.reshape(images, tokens, head_count, head_size)
    scores = (
        jnp.einsum("ithd,iphd->ithp", query_heads, key_heads, preferred_element_type=jnp.float32)
        * score_scale
    )
    block_ids = (offset + jnp.arange(tokens, dtype=jnp.int32)) // BLOCK
    phrase_ids = jnp.arange(slot_count, dtype=jnp.int32)
    visible = (
        (phrase_ids[None, None, :] < phrase_counts[:, None, None])
        & (region_first[:, None, :] <= block_ids[None, :, None])
        & (block_ids[None, :, None] <= region_last[:, None, :])
    )
    scores = jnp.where(visible[:, :, None, :], scores, -jnp.inf)
    row_max = jnp.max(scores, axis=-1, keepdims=True)
    exponent = jnp.exp(scores - row_max)
    attn_probs = exponent / jnp.sum(exponent, axis=-1, keepdims=True)
    probs_low = attn_probs.astype(jnp.bfloat16)
    prob_grad = jnp.einsum(
        "ithd,iphd->ithp", grad_heads, value_heads, preferred_element_type=jnp.float32
    )
    inner_sum = jnp.sum(attn_probs * prob_grad, axis=-1, keepdims=True)
    score_grad = (attn_probs * (prob_grad - inner_sum) * score_scale).astype(jnp.bfloat16)
    query_grad = jnp.einsum(
        "ithp,iphd->ithd", score_grad, key_heads, preferred_element_type=jnp.float32
    ).astype(jnp.bfloat16)
    latent_grad = times_transposed(
        query_grad.reshape(images * tokens, features), query_weight
    ).astype(jnp.bfloat16)
    key_part = jnp.einsum(
        "ithp,ithd->iphd", score_grad, query_heads, preferred_element_type=jnp.float32
    ).reshape(images, slot_count, features)
    value_part = jnp.einsum(
        "ithp,ithd->iphd", probs_low, grad_heads, preferred_element_type=jnp.float32
    ).reshape(images, slot_count, features)
    return (latent_grad.reshape(images, tokens, features), key_part, value_part)


def plain(
    latents,
    out_grad,
    phrases,
    query_weight,
    key_weight,
    value_weight,
    first_weight,
    second_weight,
    region_first,
    region_last,
    phrase_counts,
):
    images, tokens, features = latents.shape
    slot_count = phrases.shape[1]
    shard_rows = first_weight.shape[0]
    col_start = lax.axis_index("seq") * shard_rows
    phrase_rows = phrases.reshape(images * slot_count, features)

    def own_cols(matrix):
        return lax.dynamic_slice_in_dim(matrix, col_start, shard_rows, 1)

    full_first, full_second, full_key, full_value = (
        lax.all_gather(first_weight, "seq", axis=0, tiled=True),
        lax.all_gather(second_weight, "seq", axis=0, tiled=True),
        lax.all_gather(key_weight, "seq", axis=0, tiled=True),
        lax.all_gather(value_weight, "seq", axis=0, tiled=True),
    )
    pre_act = jnp.dot(phrase_rows, full_first, preferred_element_type=jnp.float32)
    hidden = jax.nn.silu(pre_act).astype(jnp.bfloat16)
    encoded = jnp.dot(hidden, full_second, preferred_element_type=jnp.float32).astype(jnp.bfloat16)
    key_rows = jnp.dot(encoded, full_key, preferred_element_type=jnp.float32).astype(jnp.bfloat16)
    value_rows = jnp.dot(encoded, full_value, preferred_element_type=jnp.float32).astype(
        jnp.bfloat16
    )
    offset = lax.axis_index("seq") * tokens
    latent_grad, key_part, value_part = attention_grads(
        latents,
        out_grad,
        query_weight,
        key_rows.reshape(images, slot_count, features),
        value_rows.reshape(images, slot_count, features),
        region_first,
        region_last,
        phrase_counts,
        offset,
    )
    key_sum_grad, value_sum_grad = lax.psum((key_part, value_part), "seq")
    key_grad = key_sum_grad.astype(jnp.bfloat16).reshape(images * slot_count, features)
    value_grad = value_sum_grad.astype(jnp.bfloat16).reshape(images * slot_count, features)
    encoded_grad = (
        times_transposed(key_grad, full_key) + times_transposed(value_grad, full_value)
    ).astype(jnp.bfloat16)
    second_grad = transposed_times(own_cols(hidden), encoded_grad)
    hidden_grad = times_transposed(encoded_grad, full_second)
    act_grad = (hidden_grad * silu_slope(pre_act)).astype(jnp.bfloat16)
    first_grad = transposed_times(own_cols(phrase_rows), act_grad)
    phrase_grad = times_transposed(act_grad, full_first).astype(jnp.bfloat16)
    first_grad, second_grad = lax.psum((first_grad, second_grad), "dp")
    return (latent_grad, phrase_grad.reshape(images, slot_count, features), first_grad, second_grad)


def local(shards, planes, *args):
    shard_rows = args[6].shape[0]
    if shard_rows % 16:
        return plain(*args)
    return tiled(shards, planes, *args)


def tiled(
    shards,
    planes,
    latents,
    out_grad,
    phrases,
    query_weight,
    key_weight,
    value_weight,
    first_weight,
    second_weight,
    region_first,
    region_last,
    phrase_counts,
):
    images, tokens, features = latents.shape
    slots = phrases.shape[1]
    shard_rows = first_weight.shape[0]
    chips = shards // 2
    rows = images * slots
    half = rows // 2
    shard, plane = lax.axis_index("seq"), lax.axis_index("dp")
    core = shard % 2
    place = jnp.stack([shard // 2, core, plane % 2]).astype(jnp.int32)
    shape = jax.ShapeDtypeStruct

    def swap(array, distance):
        return lax.ppermute(array, "seq", [(i, i ^ distance) for i in range(shards)])

    def swap_by_plane(array, even, odd):
        pairs = [
            (p * shards + i, p * shards + (i ^ (2 * (odd if p % 2 else even))))
            for p in range(planes)
            for i in range(shards)
        ]
        return lax.ppermute(array, ("dp", "seq"), pairs)

    def chip_peers(array):
        return [swap(array, 2 * k) for k in range(1, chips)]

    def plane_swap(array, distance):
        return lax.ppermute(array, "dp", [(i, i ^ distance) for i in range(planes)])

    def plane_peers(array):
        return [plane_swap(array, k) for k in range(1, planes)]

    def after_all(parts, *others):
        return lax.optimization_barrier((*parts, *others))[: len(parts)]

    def after(array, *others):
        return lax.optimization_barrier((array, *others))[0]

    def with_other_core(blocks):
        return blocks + [swap(block, 1) for block in blocks]

    def total_of(parts):
        return functools.reduce(jnp.add, [part.astype(jnp.float32) for part in parts])

    def project_queries(tokens_in):
        return jnp.dot(
            tokens_in.reshape(images * tokens, features),
            query_weight,
            preferred_element_type=jnp.float32,
        ).astype(jnp.bfloat16)

    phrase_rows = phrases.reshape(rows, features)
    bias = visible_bias(region_first, region_last, phrase_counts, shard * tokens, tokens)
    weight_shape = pltpu.VMEM((features, features), jnp.bfloat16)
    sum_shape = pltpu.VMEM((rows, features), jnp.float32)
    def join(parts, lengths, whole_rows):
        return pl.pallas_call(
            join_kernel,
            out_shape=[shape((whole_rows, features), jnp.bfloat16)] * lengths,
            in_specs=[VMEM] * len(parts),
            out_specs=[VMEM] * lengths,
            name="join",
        )(*parts)

    encoder, projector = join(
        [first_weight, second_weight, key_weight, value_weight], 2, 2 * shard_rows
    )
    if chips == 4:
        encoder_near = swap_by_plane(encoder, 1, 2)
        projector_near = swap_by_plane(projector, 2, 1)
        encoder_own, projector_own = swap(encoder, 1), swap(projector, 1)
        own_half = lax.dynamic_slice_in_dim(
            after(phrase_rows, encoder_own, projector_own), core * half, half, 0
        )
        queries = project_queries(after(latents, encoder_own, projector_own))
        plane_phrases = plane_peers(own_half)
        far_phrases = [swap(part, 1) for part in after_all(plane_phrases, queries)]
        encoder_next, projector_near, far_phrases, queries, bias, place = (
            lax.optimization_barrier(
                (encoder_near, projector_near, far_phrases, queries, bias, place)
            )
        )
        key_third, value_third = [
            swap_by_plane(block, 1, 2) for block in (key_weight, value_weight)
        ]
        encoder_far = swap_by_plane(encoder_next, 2, 1)
        encoder_third = plane_swap(encoder_next, 1)
        key_near = projector_near[:shard_rows]
        pairs = [swap(after(encoder_next, key_near), 1), swap(projector_near, 1)]
        key_far = swap_by_plane(after(key_near, value_third), 1, 2)
        value_far = swap_by_plane(value_third, 2, 1)
        arrays = [encoder, encoder_near, projector, projector_near]
        arrays += [encoder_far, encoder_third, key_third, value_third, key_far, value_far]
        arrays += [encoder_own, pairs[0], projector_own, pairs[1]]
        early = after_all([encoder_far, encoder_third], key_third, value_third)
        arrays += [swap(block, 1) for block in (*early, key_third, value_third)]
        layout = {
            "first": (0, [(0, 0), (1, 0), (5, 0), (4, 0)]),
            "second": (0, [(i, shard_rows) for i in (0, 1, 5, 4)]),
            "key": (1, [(2, 0), (3, 0), (6, 0), (8, 0)]),
            "value": (1, [(2, shard_rows), (3, shard_rows), (7, 0), (9, 0)]),
        }
    else:
        own_half = lax.dynamic_slice_in_dim(phrase_rows, core * half, half, 0)
        plane_phrases = plane_peers(own_half)
        far_phrases = [swap(part, 1) for part in plane_phrases]
        queries = project_queries(latents)
        arrays = [encoder] + chip_peers(encoder) + [projector] + chip_peers(projector)
        arrays += [swap(block, 1) for block in arrays]
        layout = {
            name: (0, [(first + k, offset) for k in range(chips)])
            for name, first, offset in (
                ("first", 0, 0),
                ("second", 0, shard_rows),
                ("key", chips, 0),
                ("value", chips, shard_rows),
            )
        }
    near_count = chips == 4 and 10 or len(arrays) // 2
    for name, (scheme, blocks) in layout.items():
        layout[name] = (scheme, blocks + [(near_count + i, offset) for i, offset in blocks])

    def weights(*names):
        used = sorted({i for name in names for i, _ in layout[name][1]})
        own_layout = {
            name: (layout[name][0], [(used.index(i), offset) for i, offset in layout[name][1]])
            for name in names
        }
        return [arrays[i] for i in used], {**own_layout, "arrays": len(used)}

    all_rows = planes * rows
    encoder_arrays, encoder_layout = weights("first", "second")
    encoded, slope, own_hidden, own_phrases, whole_first, whole_second = pl.pallas_call(
        functools.partial(encode_kernel, chips, planes, encoder_layout),
        out_shape=[
            shape((rows, features), jnp.bfloat16),
            shape((all_rows, features), jnp.float32),
            shape((all_rows, shard_rows), jnp.bfloat16),
            shape((all_rows, shard_rows), jnp.bfloat16),
            shape((features, features), jnp.bfloat16),
            shape((features, features), jnp.bfloat16),
        ],
        in_specs=[SMEM] + [VMEM] * (2 * planes - 1 + len(encoder_arrays)),
        out_specs=[VMEM] * 6,
        scratch_shapes=[pltpu.VMEM((all_rows, features), jnp.bfloat16)],
        compiler_params=vmem(18),
        cost_estimate=pl.CostEstimate(
            flops=10**6, bytes_accessed=10**4, transcendentals=0
        ),
        name="encode",
    )(place, phrase_rows, *plane_phrases, *far_phrases, *encoder_arrays)
    grads = out_grad.reshape(images * tokens, features)
    if chips == 4:
        *late, encoded = lax.optimization_barrier((*arrays[8:10], encoded))
        arrays[8:10] = late
        arrays += [swap(block, 1) for block in late]
    projector_arrays, projector_layout = weights("key", "value")
    key_rows, score_grad, grad_mine, grad_other = pl.pallas_call(
        functools.partial(attend_kernel, chips, images, projector_layout),
        out_shape=[
            shape((rows, features), jnp.bfloat16),
            shape((images, H * slots, tokens), jnp.bfloat16),
            shape((half, features), jnp.float32),
            shape((half, features), jnp.float32),
        ],
        in_specs=[SMEM] + [VMEM] * (len(projector_arrays) + 4),
        out_specs=[VMEM] * 4,
        scratch_shapes=[
            weight_shape,
            weight_shape,
            pltpu.VMEM((rows, features), jnp.bfloat16),
            sum_shape,
            sum_shape,
            sum_shape,
        ],
        compiler_params=vmem(28),
        cost_estimate=pl.CostEstimate(
            flops=10**10, bytes_accessed=12 * 10**6, transcendentals=10**6
        ),
        name="attend",
    )(place, encoded, *projector_arrays, queries, grads, bias)

    def latent_part(image, scores_in, whole=None):
        given = [] if whole is None else [whole]
        kernel = functools.partial(latent_kernel, image)
        return pl.pallas_call(
            kernel if whole is None else lambda _, *refs: kernel(*refs),
            out_shape=shape((images * tokens, features), jnp.bfloat16),
            in_specs=[ANY] * len(given) + [VMEM] * 3,
            out_specs=ANY,
            scratch_shapes=[
                pltpu.VMEM((tokens, features), jnp.bfloat16),
                pltpu.SemaphoreType.DMA((2,)),
            ],
            input_output_aliases={0: 0} if given else {},
            compiler_params=vmem(12),
            cost_estimate=pl.CostEstimate(
                flops=3 * 10**9, bytes_accessed=4 * 10**6, transcendentals=0
            ),
            name="latent",
        )(*given, scores_in, key_rows, query_weight)

    grad_pair = total_of([grad_mine, swap(grad_other, 1)]).astype(jnp.bfloat16)
    grad_own = total_of([grad_pair] + chip_peers(grad_pair)).astype(jnp.bfloat16)
    latent_grad = latent_part(0, score_grad)
    grad_own, latent_grad = lax.optimization_barrier((grad_own, latent_grad))
    for image in range(1, images):
        latent_grad = latent_part(image, score_grad, latent_grad)
    grad_mines = [grad_own] + plane_peers(grad_own)
    grad_fars = [swap(grad_own, 1)]
    grad_fars += [swap(part, 1) for part in after_all(grad_mines[1:], latent_grad)]
    second_grad, first_grad, phrase_grad = pl.pallas_call(
        functools.partial(weight_grad_kernel, planes),
        out_shape=[
            shape((shard_rows, features), jnp.float32),
            shape((shard_rows, features), jnp.float32),
            shape((rows, features), jnp.bfloat16),
        ],
        in_specs=[SMEM] + [VMEM] * (2 * planes + 5),
        out_specs=[ANY, ANY, VMEM],
        scratch_shapes=[
            pltpu.VMEM((all_rows, features), jnp.bfloat16),
            pltpu.VMEM((shard_rows, features), jnp.float32),
            pltpu.VMEM((shard_rows, features), jnp.float32),
            pltpu.SemaphoreType.DMA((2,)),
        ],
        compiler_params=vmem(20),
        name="weight_grads",
    )(
        place,
        *grad_mines,
        *grad_fars,
        whole_first,
        whole_second,
        slope,
        own_hidden,
        own_phrases,
    )
    return (
        latent_grad.reshape(images, tokens, features),
        phrase_grad.reshape(images, slots, features),
        first_grad,
        second_grad,
    )


def solution(mesh):
    shards, planes = mesh.shape["seq"], mesh.shape["dp"]
    in_specs = (
        P("dp", "seq", None),
        P("dp", "seq", None),
        P("dp", None, None),
        P(),
        P("seq", None),
        P("seq", None),
        P("seq", None),
        P("seq", None),
        P("dp", None),
        P("dp", None),
        P("dp"),
    )
    out_specs = (P("dp", "seq", None), P("dp", None, None), P("seq", None), P("seq", None))
    return jax.shard_map(
        functools.partial(local, shards, planes),
        mesh=mesh,
        in_specs=in_specs,
        out_specs=out_specs,
        check_vma=False,
    )
```

```python
import functools

import jax
import jax.numpy as jnp
from jax import lax
from jax.experimental import pallas as pl
from jax.experimental.pallas import tpu as pltpu
from jax.sharding import PartitionSpec as P

H = 16
BLOCK = 128
GROUP = 8
VMEM = pl.BlockSpec(memory_space=pltpu.VMEM)
SMEM = pl.BlockSpec(memory_space=pltpu.SMEM)
ANY = pl.BlockSpec(memory_space=pl.ANY)


def vmem(mebibytes):
    return pltpu.CompilerParams(vmem_limit_bytes=mebibytes * 1024 * 1024)


def silu_slope(pre_act):
    sigmoid = jax.nn.sigmoid(pre_act)
    return sigmoid * (1.0 + pre_act * (1.0 - sigmoid))


def contract(left_arg, right_arg, left_dim, right_dim):
    return lax.dot_general(
        left_arg,
        right_arg,
        (((left_dim,), (right_dim,)), ((), ())),
        preferred_element_type=jnp.float32,
    )


def times_transposed(left_arg, right_arg):
    return contract(left_arg, right_arg, 1, 1)


def transposed_times(left_arg, right_arg):
    return contract(left_arg, right_arg, 0, 0)


def split_times_transposed(left_arg, right_arg):
    rows = left_arg.shape[0]
    high = left_arg.astype(jnp.bfloat16)
    low = (left_arg - high.astype(jnp.float32)).astype(jnp.bfloat16)
    product = times_transposed(jnp.concatenate([high, low], axis=0), right_arg)
    return product[:rows] + product[rows:]


def visible_bias(region_first, region_last, phrase_counts, offset, tokens):
    block_ids = (offset + jnp.arange(tokens, dtype=jnp.int32)) // BLOCK
    phrase_ids = jnp.arange(region_first.shape[1], dtype=jnp.int32)
    visible = (
        (phrase_ids[None, :, None] < phrase_counts[:, None, None])
        & (region_first[:, :, None] <= block_ids[None, None, :])
        & (block_ids[None, None, :] <= region_last[:, :, None])
    )
    return jnp.where(visible, 0.0, -jnp.inf).astype(jnp.float32)


def window(group, head_size):
    start = group * GROUP * head_size
    return start // 128 * 128, -(-(start + GROUP * head_size) // 128) * 128


def own_columns(rows, group, head, head_size, low):
    first = (group * GROUP + head) * head_size - low
    column = lax.broadcasted_iota(jnp.int32, rows.shape, 1)
    return jnp.where((column >= first) & (column < first + head_size), rows, jnp.zeros_like(rows))


def block_diagonal(rows, group, head_size, low):
    return jnp.concatenate(
        [own_columns(rows, group, head, head_size, low) for head in range(GROUP)], axis=0
    )


def block_places(place_ref, scheme, chips):
    chip, core, odd = place_ref[0], place_ref[1], place_ref[2]
    steps = list(range(chips))
    if chips == 4:
        turn = odd if scheme == 0 else 1 - odd
        steps = [0, 1 + turn, 2 - turn, 3]
    return [2 * (chip ^ step) + other for other in (core, 1 - core) for step in steps]


def load_weight(name, layout, arrays, place_ref, chips, whole):
    scheme, blocks = layout[name]
    rows = whole.shape[0] // len(blocks)
    for (array, offset), place in zip(blocks, block_places(place_ref, scheme, chips)):
        whole[pl.ds(pl.multiple_of(place * rows, 16), rows)] = arrays[array][offset : offset + rows]


def project(left_arg, right_arg):
    return jnp.dot(left_arg, right_arg, preferred_element_type=jnp.float32)


def join_kernel(*refs):
    outs = [ref for ref in refs if ref.shape[0] == max(r.shape[0] for r in refs)]
    parts = iter(refs[: len(refs) - len(outs)])
    for out in outs:
        start = 0
        while start < out.shape[0]:
            part = next(parts)
            stop = min(start + part.shape[0], out.shape[0])
            out[start:stop] = part[: stop - start]
            start = stop


def join_halves(out_ref, core, start, mine, far):
    half = mine[0].shape[0]
    for plane in range(len(mine)):
        first = start + plane * 2 * half
        out_ref[pl.ds(pl.multiple_of(first + core * half, 16), half)] = mine[plane][...]
        out_ref[pl.ds(pl.multiple_of(first + (1 - core) * half, 16), half)] = far[plane][...]


def wait_all(copies):
    for copy in copies:
        copy.wait()


def encode_kernel(chips, planes, layout, place_ref, phrase_ref, *refs):
    others = planes - 1
    mine, far = refs[:others], refs[others : 2 * others]
    arrays = refs[2 * others : 2 * others + layout["arrays"]]
    (
        encoded_out,
        slope_out,
        own_hidden_out,
        own_phrase_out,
        first_weight,
        second_weight,
        phrases,
    ) = refs[2 * others + layout["arrays"] :]
    own_rows = phrase_ref.shape[0]
    phrases[:own_rows] = phrase_ref[...]
    join_halves(phrases, place_ref[1], own_rows, mine, far)
    load_weight("first", layout, arrays, place_ref, chips, first_weight)
    load_weight("second", layout, arrays, place_ref, chips, second_weight)
    columns = own_phrase_out.shape[1]
    selected = lax.broadcasted_iota(jnp.int32, (phrases.shape[1], columns), 0)
    selected -= (2 * place_ref[0] + place_ref[1]) * columns
    select = selected == lax.broadcasted_iota(jnp.int32, selected.shape, 1)
    select = jnp.where(select, 1.0, 0.0).astype(jnp.bfloat16)
    own_phrase_out[...] = project(phrases[...], select).astype(jnp.bfloat16)
    pre_act = project(phrases[...], first_weight[...])
    sigmoid = jax.nn.sigmoid(pre_act)
    hidden = (pre_act * sigmoid).astype(jnp.bfloat16)
    slope_out[...] = sigmoid * (1.0 + pre_act * (1.0 - sigmoid))
    own_hidden_out[...] = project(hidden, select).astype(jnp.bfloat16)
    encoded_out[...] = project(hidden[:own_rows], second_weight[...]).astype(jnp.bfloat16)


def query_kernel(token_ref, weight_ref, out_ref):
    out_ref[...] = project(token_ref[...], weight_ref[...]).astype(jnp.bfloat16)


def head_parts(slots):
    return [slice(head * slots, (head + 1) * slots) for head in range(GROUP)]


def own_head_sum(full, group, head_size, low):
    slots = full.shape[0] // GROUP
    return functools.reduce(
        jnp.add,
        [
            own_columns(full[part], group, head, head_size, low)
            for head, part in enumerate(head_parts(slots))
        ],
    )


def attend_kernel(chips, images, layout, place_ref, encoded_ref, *refs):
    arrays = refs[: layout["arrays"]]
    (
        query,
        grad,
        bias_ref,
        key_out,
        score_out,
        mine_out,
        other_out,
        key_weight,
        value_weight,
        value_rows,
        key_sum,
        value_sum,
        total,
    ) = refs[layout["arrays"] :]
    own_rows = encoded_ref.shape[0]
    load_weight("key", layout, arrays, place_ref, chips, key_weight)
    load_weight("value", layout, arrays, place_ref, chips, value_weight)
    key_out[...] = project(encoded_ref[...], key_weight[...]).astype(jnp.bfloat16)
    value_rows[...] = project(encoded_ref[...], value_weight[...]).astype(jnp.bfloat16)

    slots = own_rows // images
    features = query.shape[1]
    tokens = query.shape[0] // images
    head_size = features // H
    scale = head_size ** (-0.5)
    key_sum[...] = jnp.zeros_like(key_sum)
    value_sum[...] = jnp.zeros_like(value_sum)
    for image in range(images):
        rows = pl.ds(image * slots, slots)
        here = pl.ds(image * tokens, tokens)
        bias = bias_ref[image]
        for group in range(H // GROUP):
            low, high = window(group, head_size)
            columns = pl.ds(low, high - low)
            keys = block_diagonal(key_out[rows, columns], group, head_size, low)
            values = block_diagonal(value_rows[rows, columns], group, head_size, low)
            queries = query[here, columns]
            grads = grad[here, columns]
            scores = times_transposed(keys, queries)
            prob_grad = times_transposed(values, grads)
            probs_low, score_grad = [], []
            for part in head_parts(slots):
                score = scores[part] * scale + bias
                exponent = jnp.exp(score - jnp.max(score, axis=0, keepdims=True))
                probs = exponent * (1.0 / jnp.sum(exponent, axis=0, keepdims=True))
                upstream = prob_grad[part]
                inner = jnp.sum(probs * upstream, axis=0, keepdims=True)
                probs_low.append(probs.astype(jnp.bfloat16))
                score_grad.append((probs * (upstream - inner) * scale).astype(jnp.bfloat16))
            probs_low = jnp.concatenate(probs_low, axis=0)
            score_grad = jnp.concatenate(score_grad, axis=0)
            score_out[image, pl.ds(group * GROUP * slots, GROUP * slots)] = score_grad
            key_sum[rows, columns] += own_head_sum(
                project(score_grad, queries), group, head_size, low
            )
            value_sum[rows, columns] += own_head_sum(
                project(probs_low, grads), group, head_size, low
            )
    total[...] = split_times_transposed(key_sum[...], key_weight[...]) + split_times_transposed(
        value_sum[...], value_weight[...]
    )
    core = place_ref[1]
    half = mine_out.shape[0]
    mine_out[...] = total[pl.ds(pl.multiple_of(core * half, 8), half)]
    other_out[...] = total[pl.ds(pl.multiple_of((1 - core) * half, 8), half)]


def latent_kernel(image, score_ref, key_ref, weight, out_ref, result, out_sem):
    slots, features = key_ref.shape[0] // score_ref.shape[0], weight.shape[0]
    tokens = score_ref.shape[2]
    head_size = features // H
    parts = []
    for group in range(H // GROUP):
        low, high = window(group, head_size)
        rows = key_ref[image * slots : (image + 1) * slots, low:high]
        keys = block_diagonal(rows, group, head_size, low)
        score_grad = score_ref[image, group * GROUP * slots : (group + 1) * GROUP * slots]
        part = transposed_times(score_grad, keys)
        if low:
            part = jnp.concatenate([jnp.zeros((part.shape[0], low), jnp.float32), part], axis=1)
        if high < features:
            part = jnp.concatenate(
                [part, jnp.zeros((part.shape[0], features - high), jnp.float32)], axis=1
            )
        parts.append(part)
    query_grad = functools.reduce(jnp.add, parts).astype(jnp.bfloat16)
    tile = tokens // out_sem.shape[0]
    copies = []
    for step in range(out_sem.shape[0]):
        rows = slice(step * tile, (step + 1) * tile)
        result[rows] = times_transposed(query_grad[rows], weight[...]).astype(jnp.bfloat16)
        copies.append(
            pltpu.make_async_copy(
                result.at[rows], out_ref.at[pl.ds(image * tokens + step * tile, tile)], out_sem.at[step]
            )
        )
        copies[-1].start()
    wait_all(copies)


def weight_grad_kernel(planes, place_ref, *refs):
    mine, far = refs[:planes], refs[planes : 2 * planes]
    (
        first_weight,
        second_weight,
        slope_ref,
        hidden_ref,
        phrase_ref,
        second_out,
        first_out,
        phrase_out,
        encoded_grad,
        second_grad,
        first_grad,
        out_sem,
    ) = refs[2 * planes :]
    join_halves(encoded_grad, place_ref[1], 0, mine, far)
    second_grad[...] = transposed_times(hidden_ref[...], encoded_grad[...])
    second_copy = pltpu.make_async_copy(second_grad, second_out, out_sem.at[0])
    second_copy.start()
    hidden_grad = times_transposed(encoded_grad[...], second_weight[...])
    act_grad = (hidden_grad * slope_ref[...]).astype(jnp.bfloat16)
    first_grad[...] = transposed_times(phrase_ref[...], act_grad)
    first_copy = pltpu.make_async_copy(first_grad, first_out, out_sem.at[1])
    first_copy.start()
    phrase_out[...] = times_transposed(
        act_grad[: phrase_out.shape[0]], first_weight[...]
    ).astype(jnp.bfloat16)
    second_copy.wait()
    first_copy.wait()


def attention_grads(
    latents,
    out_grad,
    query_weight,
    key_rows,
    value_rows,
    region_first,
    region_last,
    phrase_counts,
    offset,
):
    images, tokens, features = latents.shape
    slot_count = key_rows.shape[1]
    head_count = H
    head_size = features // head_count
    score_scale = head_size ** (-0.5)
    queries = jnp.dot(
        latents.reshape(images * tokens, features), query_weight, preferred_element_type=jnp.float32
    ).astype(jnp.bfloat16)
    query_heads = queries.reshape(images, tokens, head_count, head_size)
    key_heads = key_rows.reshape(images, slot_count, head_count, head_size)
    value_heads = value_rows.reshape(images, slot_count, head_count, head_size)
    grad_heads = out_grad.reshape(images, tokens, head_count, head_size)
    scores = (
        jnp.einsum("ithd,iphd->ithp", query_heads, key_heads, preferred_element_type=jnp.float32)
        * score_scale
    )
    block_ids = (offset + jnp.arange(tokens, dtype=jnp.int32)) // BLOCK
    phrase_ids = jnp.arange(slot_count, dtype=jnp.int32)
    visible = (
        (phrase_ids[None, None, :] < phrase_counts[:, None, None])
        & (region_first[:, None, :] <= block_ids[None, :, None])
        & (block_ids[None, :, None] <= region_last[:, None, :])
    )
    scores = jnp.where(visible[:, :, None, :], scores, -jnp.inf)
    row_max = jnp.max(scores, axis=-1, keepdims=True)
    exponent = jnp.exp(scores - row_max)
    attn_probs = exponent / jnp.sum(exponent, axis=-1, keepdims=True)
    probs_low = attn_probs.astype(jnp.bfloat16)
    prob_grad = jnp.einsum(
        "ithd,iphd->ithp", grad_heads, value_heads, preferred_element_type=jnp.float32
    )
    inner_sum = jnp.sum(attn_probs * prob_grad, axis=-1, keepdims=True)
    score_grad = (attn_probs * (prob_grad - inner_sum) * score_scale).astype(jnp.bfloat16)
    query_grad = jnp.einsum(
        "ithp,iphd->ithd", score_grad, key_heads, preferred_element_type=jnp.float32
    ).astype(jnp.bfloat16)
    latent_grad = times_transposed(
        query_grad.reshape(images * tokens, features), query_weight
    ).astype(jnp.bfloat16)
    key_part = jnp.einsum(
        "ithp,ithd->iphd", score_grad, query_heads, preferred_element_type=jnp.float32
    ).reshape(images, slot_count, features)
    value_part = jnp.einsum(
        "ithp,ithd->iphd", probs_low, grad_heads, preferred_element_type=jnp.float32
    ).reshape(images, slot_count, features)
    return (latent_grad.reshape(images, tokens, features), key_part, value_part)


def plain(
    latents,
    out_grad,
    phrases,
    query_weight,
    key_weight,
    value_weight,
    first_weight,
    second_weight,
    region_first,
    region_last,
    phrase_counts,
):
    images, tokens, features = latents.shape
    slot_count = phrases.shape[1]
    shard_rows = first_weight.shape[0]
    col_start = lax.axis_index("seq") * shard_rows
    phrase_rows = phrases.reshape(images * slot_count, features)

    def own_cols(matrix):
        return lax.dynamic_slice_in_dim(matrix, col_start, shard_rows, 1)

    full_first, full_second, full_key, full_value = (
        lax.all_gather(first_weight, "seq", axis=0, tiled=True),
        lax.all_gather(second_weight, "seq", axis=0, tiled=True),
        lax.all_gather(key_weight, "seq", axis=0, tiled=True),
        lax.all_gather(value_weight, "seq", axis=0, tiled=True),
    )
    pre_act = jnp.dot(phrase_rows, full_first, preferred_element_type=jnp.float32)
    hidden = jax.nn.silu(pre_act).astype(jnp.bfloat16)
    encoded = jnp.dot(hidden, full_second, preferred_element_type=jnp.float32).astype(jnp.bfloat16)
    key_rows = jnp.dot(encoded, full_key, preferred_element_type=jnp.float32).astype(jnp.bfloat16)
    value_rows = jnp.dot(encoded, full_value, preferred_element_type=jnp.float32).astype(
        jnp.bfloat16
    )
    offset = lax.axis_index("seq") * tokens
    latent_grad, key_part, value_part = attention_grads(
        latents,
        out_grad,
        query_weight,
        key_rows.reshape(images, slot_count, features),
        value_rows.reshape(images, slot_count, features),
        region_first,
        region_last,
        phrase_counts,
        offset,
    )
    key_sum_grad, value_sum_grad = lax.psum((key_part, value_part), "seq")
    key_grad = key_sum_grad.astype(jnp.bfloat16).reshape(images * slot_count, features)
    value_grad = value_sum_grad.astype(jnp.bfloat16).reshape(images * slot_count, features)
    encoded_grad = (
        times_transposed(key_grad, full_key) + times_transposed(value_grad, full_value)
    ).astype(jnp.bfloat16)
    second_grad = transposed_times(own_cols(hidden), encoded_grad)
    hidden_grad = times_transposed(encoded_grad, full_second)
    act_grad = (hidden_grad * silu_slope(pre_act)).astype(jnp.bfloat16)
    first_grad = transposed_times(own_cols(phrase_rows), act_grad)
    phrase_grad = times_transposed(act_grad, full_first).astype(jnp.bfloat16)
    first_grad, second_grad = lax.psum((first_grad, second_grad), "dp")
    return (latent_grad, phrase_grad.reshape(images, slot_count, features), first_grad, second_grad)


def local(shards, planes, *args):
    shard_rows = args[6].shape[0]
    if shard_rows % 16:
        return plain(*args)
    return tiled(shards, planes, *args)


def tiled(
    shards,
    planes,
    latents,
    out_grad,
    phrases,
    query_weight,
    key_weight,
    value_weight,
    first_weight,
    second_weight,
    region_first,
    region_last,
    phrase_counts,
):
    images, tokens, features = latents.shape
    slots = phrases.shape[1]
    shard_rows = first_weight.shape[0]
    chips = shards // 2
    rows = images * slots
    half = rows // 2
    shard, plane = lax.axis_index("seq"), lax.axis_index("dp")
    core = shard % 2
    place = jnp.stack([shard // 2, core, plane % 2]).astype(jnp.int32)
    shape = jax.ShapeDtypeStruct

    def swap(array, distance):
        return lax.ppermute(array, "seq", [(i, i ^ distance) for i in range(shards)])

    def swap_by_plane(array, even, odd):
        pairs = [
            (p * shards + i, p * shards + (i ^ (2 * (odd if p % 2 else even))))
            for p in range(planes)
            for i in range(shards)
        ]
        return lax.ppermute(array, ("dp", "seq"), pairs)

    def chip_peers(array):
        return [swap(array, 2 * k) for k in range(1, chips)]

    def plane_swap(array, distance):
        return lax.ppermute(array, "dp", [(i, i ^ distance) for i in range(planes)])

    def plane_peers(array):
        return [plane_swap(array, k) for k in range(1, planes)]

    def after_all(parts, *others):
        return lax.optimization_barrier((*parts, *others))[: len(parts)]

    def after(array, *others):
        return lax.optimization_barrier((array, *others))[0]

    def with_other_core(blocks):
        return blocks + [swap(block, 1) for block in blocks]

    def total_of(parts):
        return functools.reduce(jnp.add, [part.astype(jnp.float32) for part in parts])

    def project_queries(tokens_in):
        return pl.pallas_call(
            query_kernel,
            out_shape=shape((images * tokens, features), jnp.bfloat16),
            grid=(images * tokens // 256,),
            in_specs=[
                pl.BlockSpec((256, features), lambda t: (t, 0)),
                pl.BlockSpec((features, features), lambda t: (0, 0)),
            ],
            out_specs=pl.BlockSpec((256, features), lambda t: (t, 0)),
            compiler_params=vmem(12),
            cost_estimate=pl.CostEstimate(
                flops=3 * 10**9, bytes_accessed=8 * 10**6, transcendentals=0
            ),
            name="queries",
        )(tokens_in.reshape(images * tokens, features), query_weight)

    phrase_rows = phrases.reshape(rows, features)
    bias = visible_bias(region_first, region_last, phrase_counts, shard * tokens, tokens)
    weight_shape = pltpu.VMEM((features, features), jnp.bfloat16)
    sum_shape = pltpu.VMEM((rows, features), jnp.float32)
    def join(parts, lengths, whole_rows):
        return pl.pallas_call(
            join_kernel,
            out_shape=[shape((whole_rows, features), jnp.bfloat16)] * lengths,
            in_specs=[VMEM] * len(parts),
            out_specs=[VMEM] * lengths,
            name="join",
        )(*parts)

    encoder, projector = join(
        [first_weight, second_weight, key_weight, value_weight], 2, 2 * shard_rows
    )
    if chips == 4:
        encoder_near = swap_by_plane(encoder, 1, 2)
        projector_near = swap_by_plane(projector, 2, 1)
        encoder_own, projector_own = swap(encoder, 1), swap(projector, 1)
        own_half = lax.dynamic_slice_in_dim(
            after(phrase_rows, encoder_own, projector_own), core * half, half, 0
        )
        plane_phrases = plane_peers(own_half)
        far_phrases = [swap(part, 1) for part in plane_phrases]
        encoder_next, projector_near, far_phrases, bias, place = lax.optimization_barrier(
            (encoder_near, projector_near, far_phrases, bias, place)
        )
        projector_third = swap_by_plane(projector, 1, 2)
        encoder_far = swap_by_plane(encoder_next, 2, 1)
        encoder_third = plane_swap(encoder_next, 1)
        key_near = projector_near[:shard_rows]
        queries = project_queries(after(latents, key_near))
        pairs = [swap(after(encoder_next, key_near), 1), swap(projector_near, 1)]
        key_far = swap_by_plane(after(key_near, projector_third), 1, 2)
        value_far = swap_by_plane(projector_third[shard_rows:], 2, 1)
        arrays = [encoder, encoder_near, projector, projector_near]
        arrays += [encoder_far, encoder_third, projector_third, key_far, value_far]
        arrays += [encoder_own, pairs[0], projector_own, pairs[1]]
        early = after_all([encoder_far, encoder_third], projector_third, queries)
        arrays += [swap(block, 1) for block in (*early, projector_third)]
        layout = {
            "first": (0, [(0, 0), (1, 0), (5, 0), (4, 0)]),
            "second": (0, [(i, shard_rows) for i in (0, 1, 5, 4)]),
            "key": (1, [(2, 0), (3, 0), (6, 0), (7, 0)]),
            "value": (1, [(2, shard_rows), (3, shard_rows), (6, shard_rows), (8, 0)]),
        }
    else:
        own_half = lax.dynamic_slice_in_dim(phrase_rows, core * half, half, 0)
        plane_phrases = plane_peers(own_half)
        far_phrases = [swap(part, 1) for part in plane_phrases]
        queries = project_queries(latents)
        arrays = [encoder] + chip_peers(encoder) + [projector] + chip_peers(projector)
        arrays += [swap(block, 1) for block in arrays]
        layout = {
            name: (0, [(first + k, offset) for k in range(chips)])
            for name, first, offset in (
                ("first", 0, 0),
                ("second", 0, shard_rows),
                ("key", chips, 0),
                ("value", chips, shard_rows),
            )
        }
    near_count = chips == 4 and 9 or len(arrays) // 2
    for name, (scheme, blocks) in layout.items():
        layout[name] = (scheme, blocks + [(near_count + i, offset) for i, offset in blocks])

    def weights(*names):
        used = sorted({i for name in names for i, _ in layout[name][1]})
        own_layout = {
            name: (layout[name][0], [(used.index(i), offset) for i, offset in layout[name][1]])
            for name in names
        }
        return [arrays[i] for i in used], {**own_layout, "arrays": len(used)}

    all_rows = planes * rows
    encoder_arrays, encoder_layout = weights("first", "second")
    encoded, slope, own_hidden, own_phrases, whole_first, whole_second = pl.pallas_call(
        functools.partial(encode_kernel, chips, planes, encoder_layout),
        out_shape=[
            shape((rows, features), jnp.bfloat16),
            shape((all_rows, features), jnp.float32),
            shape((all_rows, shard_rows), jnp.bfloat16),
            shape((all_rows, shard_rows), jnp.bfloat16),
            shape((features, features), jnp.bfloat16),
            shape((features, features), jnp.bfloat16),
        ],
        in_specs=[SMEM] + [VMEM] * (2 * planes - 1 + len(encoder_arrays)),
        out_specs=[VMEM] * 6,
        scratch_shapes=[pltpu.VMEM((all_rows, features), jnp.bfloat16)],
        compiler_params=vmem(18),
        cost_estimate=pl.CostEstimate(
            flops=10**6, bytes_accessed=10**4, transcendentals=0
        ),
        name="encode",
    )(place, phrase_rows, *plane_phrases, *far_phrases, *encoder_arrays)
    grads = out_grad.reshape(images * tokens, features)
    if chips == 4:
        *late, encoded = lax.optimization_barrier((*arrays[7:9], encoded))
        arrays[7:9] = late
        arrays += [swap(block, 1) for block in late]
    projector_arrays, projector_layout = weights("key", "value")
    key_rows, score_grad, grad_mine, grad_other = pl.pallas_call(
        functools.partial(attend_kernel, chips, images, projector_layout),
        out_shape=[
            shape((rows, features), jnp.bfloat16),
            shape((images, H * slots, tokens), jnp.bfloat16),
            shape((half, features), jnp.float32),
            shape((half, features), jnp.float32),
        ],
        in_specs=[SMEM] + [VMEM] * (len(projector_arrays) + 4),
        out_specs=[VMEM] * 4,
        scratch_shapes=[
            weight_shape,
            weight_shape,
            pltpu.VMEM((rows, features), jnp.bfloat16),
            sum_shape,
            sum_shape,
            sum_shape,
        ],
        compiler_params=vmem(28),
        cost_estimate=pl.CostEstimate(
            flops=10**10, bytes_accessed=12 * 10**6, transcendentals=10**6
        ),
        name="attend",
    )(place, encoded, *projector_arrays, queries, grads, bias)

    def latent_part(image, scores_in, whole=None):
        given = [] if whole is None else [whole]
        kernel = functools.partial(latent_kernel, image)
        return pl.pallas_call(
            kernel if whole is None else lambda _, *refs: kernel(*refs),
            out_shape=shape((images * tokens, features), jnp.bfloat16),
            in_specs=[ANY] * len(given) + [VMEM] * 3,
            out_specs=ANY,
            scratch_shapes=[
                pltpu.VMEM((tokens, features), jnp.bfloat16),
                pltpu.SemaphoreType.DMA((2,)),
            ],
            input_output_aliases={0: 0} if given else {},
            compiler_params=vmem(12),
            cost_estimate=pl.CostEstimate(
                flops=3 * 10**9, bytes_accessed=4 * 10**6, transcendentals=0
            ),
            name="latent",
        )(*given, scores_in, key_rows, query_weight)

    grad_pair = total_of([grad_mine, swap(grad_other, 1)]).astype(jnp.bfloat16)
    grad_own = total_of([grad_pair] + chip_peers(grad_pair)).astype(jnp.bfloat16)
    latent_grad = latent_part(0, score_grad)
    grad_own, latent_grad = lax.optimization_barrier((grad_own, latent_grad))
    for image in range(1, images):
        latent_grad = latent_part(image, score_grad, latent_grad)
    grad_mines = [grad_own] + plane_peers(grad_own)
    grad_fars = [swap(grad_own, 1)]
    grad_fars += [swap(part, 1) for part in after_all(grad_mines[1:], latent_grad)]
    second_grad, first_grad, phrase_grad = pl.pallas_call(
        functools.partial(weight_grad_kernel, planes),
        out_shape=[
            shape((shard_rows, features), jnp.float32),
            shape((shard_rows, features), jnp.float32),
            shape((rows, features), jnp.bfloat16),
        ],
        in_specs=[SMEM] + [VMEM] * (2 * planes + 5),
        out_specs=[ANY, ANY, VMEM],
        scratch_shapes=[
            pltpu.VMEM((all_rows, features), jnp.bfloat16),
            pltpu.VMEM((shard_rows, features), jnp.float32),
            pltpu.VMEM((shard_rows, features), jnp.float32),
            pltpu.SemaphoreType.DMA((2,)),
        ],
        compiler_params=vmem(20),
        name="weight_grads",
    )(
        place,
        *grad_mines,
        *grad_fars,
        whole_first,
        whole_second,
        slope,
        own_hidden,
        own_phrases,
    )
    return (
        latent_grad.reshape(images, tokens, features),
        phrase_grad.reshape(images, slots, features),
        first_grad,
        second_grad,
    )


def solution(mesh):
    shards, planes = mesh.shape["seq"], mesh.shape["dp"]
    in_specs = (
        P("dp", "seq", None),
        P("dp", "seq", None),
        P("dp", None, None),
        P(),
        P("seq", None),
        P("seq", None),
        P("seq", None),
        P("seq", None),
        P("dp", None),
        P("dp", None),
        P("dp"),
    )
    out_specs = (P("dp", "seq", None), P("dp", None, None), P("seq", None), P("seq", None))
    return jax.shard_map(
        functools.partial(local, shards, planes),
        mesh=mesh,
        in_specs=in_specs,
        out_specs=out_specs,
        check_vma=False,
    )
```

```python
import functools

import jax
import jax.numpy as jnp
from jax import lax
from jax.experimental import pallas as pl
from jax.experimental.pallas import tpu as pltpu
from jax.sharding import PartitionSpec as P

H = 16
BLOCK = 128
GROUP = 8
VMEM = pl.BlockSpec(memory_space=pltpu.VMEM)
SMEM = pl.BlockSpec(memory_space=pltpu.SMEM)
ANY = pl.BlockSpec(memory_space=pl.ANY)


def vmem(mebibytes):
    return pltpu.CompilerParams(vmem_limit_bytes=mebibytes * 1024 * 1024)


def silu_slope(pre_act):
    sigmoid = jax.nn.sigmoid(pre_act)
    return sigmoid * (1.0 + pre_act * (1.0 - sigmoid))


def contract(left_arg, right_arg, left_dim, right_dim):
    return lax.dot_general(
        left_arg,
        right_arg,
        (((left_dim,), (right_dim,)), ((), ())),
        preferred_element_type=jnp.float32,
    )


def times_transposed(left_arg, right_arg):
    return contract(left_arg, right_arg, 1, 1)


def transposed_times(left_arg, right_arg):
    return contract(left_arg, right_arg, 0, 0)


def split_times_transposed(left_arg, right_arg):
    rows = left_arg.shape[0]
    high = left_arg.astype(jnp.bfloat16)
    low = (left_arg - high.astype(jnp.float32)).astype(jnp.bfloat16)
    product = times_transposed(jnp.concatenate([high, low], axis=0), right_arg)
    return product[:rows] + product[rows:]


def visible_bias(region_first, region_last, phrase_counts, offset, tokens):
    block_ids = (offset + jnp.arange(tokens, dtype=jnp.int32)) // BLOCK
    phrase_ids = jnp.arange(region_first.shape[1], dtype=jnp.int32)
    visible = (
        (phrase_ids[None, :, None] < phrase_counts[:, None, None])
        & (region_first[:, :, None] <= block_ids[None, None, :])
        & (block_ids[None, None, :] <= region_last[:, :, None])
    )
    return jnp.where(visible, 0.0, -jnp.inf).astype(jnp.float32)


def window(group, head_size):
    start = group * GROUP * head_size
    return start // 128 * 128, -(-(start + GROUP * head_size) // 128) * 128


def own_columns(rows, group, head, head_size, low):
    first = (group * GROUP + head) * head_size - low
    column = lax.broadcasted_iota(jnp.int32, rows.shape, 1)
    return jnp.where((column >= first) & (column < first + head_size), rows, jnp.zeros_like(rows))


def block_diagonal(rows, group, head_size, low):
    return jnp.concatenate(
        [own_columns(rows, group, head, head_size, low) for head in range(GROUP)], axis=0
    )


def block_places(place_ref, scheme, chips):
    chip, core, odd = place_ref[0], place_ref[1], place_ref[2]
    steps = list(range(chips))
    if chips == 4:
        turn = odd if scheme == 0 else 1 - odd
        steps = [0, 1 + turn, 2 - turn, 3]
    return [2 * (chip ^ step) + other for other in (core, 1 - core) for step in steps]


def load_weight(name, layout, arrays, place_ref, chips, whole):
    scheme, blocks = layout[name]
    rows = whole.shape[0] // len(blocks)
    for (array, offset), place in zip(blocks, block_places(place_ref, scheme, chips)):
        whole[pl.ds(pl.multiple_of(place * rows, 16), rows)] = arrays[array][offset : offset + rows]


def project(left_arg, right_arg):
    return jnp.dot(left_arg, right_arg, preferred_element_type=jnp.float32)


def join_kernel(*refs):
    outs = [ref for ref in refs if ref.shape[0] == max(r.shape[0] for r in refs)]
    parts = iter(refs[: len(refs) - len(outs)])
    for out in outs:
        start = 0
        while start < out.shape[0]:
            part = next(parts)
            stop = min(start + part.shape[0], out.shape[0])
            out[start:stop] = part[: stop - start]
            start = stop


def join_halves(out_ref, core, start, mine, far):
    half = mine[0].shape[0]
    for plane in range(len(mine)):
        first = start + plane * 2 * half
        out_ref[pl.ds(pl.multiple_of(first + core * half, 16), half)] = mine[plane][...]
        out_ref[pl.ds(pl.multiple_of(first + (1 - core) * half, 16), half)] = far[plane][...]


def wait_all(copies):
    for copy in copies:
        copy.wait()


def encode_kernel(chips, planes, layout, place_ref, phrase_ref, *refs):
    others = planes - 1
    mine, far = refs[:others], refs[others : 2 * others]
    arrays = refs[2 * others : 2 * others + layout["arrays"]]
    (
        encoded_out,
        slope_out,
        own_hidden_out,
        own_phrase_out,
        first_weight,
        second_weight,
        phrases,
    ) = refs[2 * others + layout["arrays"] :]
    own_rows = phrase_ref.shape[0]
    phrases[:own_rows] = phrase_ref[...]
    join_halves(phrases, place_ref[1], own_rows, mine, far)
    load_weight("first", layout, arrays, place_ref, chips, first_weight)
    load_weight("second", layout, arrays, place_ref, chips, second_weight)
    columns = own_phrase_out.shape[1]
    selected = lax.broadcasted_iota(jnp.int32, (phrases.shape[1], columns), 0)
    selected -= (2 * place_ref[0] + place_ref[1]) * columns
    select = selected == lax.broadcasted_iota(jnp.int32, selected.shape, 1)
    select = jnp.where(select, 1.0, 0.0).astype(jnp.bfloat16)
    own_phrase_out[...] = project(phrases[...], select).astype(jnp.bfloat16)
    pre_act = project(phrases[...], first_weight[...])
    sigmoid = jax.nn.sigmoid(pre_act)
    hidden = (pre_act * sigmoid).astype(jnp.bfloat16)
    slope_out[...] = sigmoid * (1.0 + pre_act * (1.0 - sigmoid))
    own_hidden_out[...] = project(hidden, select).astype(jnp.bfloat16)
    encoded_out[...] = project(hidden[:own_rows], second_weight[...]).astype(jnp.bfloat16)


def query_kernel(token_ref, weight_ref, out_ref):
    out_ref[...] = project(token_ref[...], weight_ref[...]).astype(jnp.bfloat16)


def head_parts(slots):
    return [slice(head * slots, (head + 1) * slots) for head in range(GROUP)]


def own_head_sum(full, group, head_size, low):
    slots = full.shape[0] // GROUP
    return functools.reduce(
        jnp.add,
        [
            own_columns(full[part], group, head, head_size, low)
            for head, part in enumerate(head_parts(slots))
        ],
    )


def attend_kernel(chips, images, layout, place_ref, encoded_ref, *refs):
    arrays = refs[: layout["arrays"]]
    (
        query,
        grad,
        bias_ref,
        key_out,
        score_out,
        mine_out,
        other_out,
        key_weight,
        value_weight,
        value_rows,
        key_sum,
        value_sum,
        total,
    ) = refs[layout["arrays"] :]
    own_rows = encoded_ref.shape[0]
    load_weight("key", layout, arrays, place_ref, chips, key_weight)
    load_weight("value", layout, arrays, place_ref, chips, value_weight)
    key_out[...] = project(encoded_ref[...], key_weight[...]).astype(jnp.bfloat16)
    value_rows[...] = project(encoded_ref[...], value_weight[...]).astype(jnp.bfloat16)

    slots = own_rows // images
    features = query.shape[1]
    tokens = query.shape[0] // images
    head_size = features // H
    scale = head_size ** (-0.5)
    key_sum[...] = jnp.zeros_like(key_sum)
    value_sum[...] = jnp.zeros_like(value_sum)
    for image in range(images):
        rows = pl.ds(image * slots, slots)
        here = pl.ds(image * tokens, tokens)
        bias = bias_ref[image]
        for group in range(H // GROUP):
            low, high = window(group, head_size)
            columns = pl.ds(low, high - low)
            keys = block_diagonal(key_out[rows, columns], group, head_size, low)
            values = block_diagonal(value_rows[rows, columns], group, head_size, low)
            queries = query[here, columns]
            grads = grad[here, columns]
            scores = times_transposed(keys, queries)
            prob_grad = times_transposed(values, grads)
            probs_low, score_grad = [], []
            for part in head_parts(slots):
                score = scores[part] * scale + bias
                exponent = jnp.exp(score - jnp.max(score, axis=0, keepdims=True))
                probs = exponent * (1.0 / jnp.sum(exponent, axis=0, keepdims=True))
                upstream = prob_grad[part]
                inner = jnp.sum(probs * upstream, axis=0, keepdims=True)
                probs_low.append(probs.astype(jnp.bfloat16))
                score_grad.append((probs * (upstream - inner) * scale).astype(jnp.bfloat16))
            probs_low = jnp.concatenate(probs_low, axis=0)
            score_grad = jnp.concatenate(score_grad, axis=0)
            score_out[image, pl.ds(group * GROUP * slots, GROUP * slots)] = score_grad
            key_sum[rows, columns] += own_head_sum(
                project(score_grad, queries), group, head_size, low
            )
            value_sum[rows, columns] += own_head_sum(
                project(probs_low, grads), group, head_size, low
            )
    total[...] = split_times_transposed(key_sum[...], key_weight[...]) + split_times_transposed(
        value_sum[...], value_weight[...]
    )
    core = place_ref[1]
    half = mine_out.shape[0]
    mine_out[...] = total[pl.ds(pl.multiple_of(core * half, 8), half)]
    other_out[...] = total[pl.ds(pl.multiple_of((1 - core) * half, 8), half)]


def latent_kernel(image, score_ref, key_ref, weight, out_ref, result, out_sem):
    slots, features = key_ref.shape[0] // score_ref.shape[0], weight.shape[0]
    tokens = score_ref.shape[2]
    head_size = features // H
    parts = []
    for group in range(H // GROUP):
        low, high = window(group, head_size)
        rows = key_ref[image * slots : (image + 1) * slots, low:high]
        keys = block_diagonal(rows, group, head_size, low)
        score_grad = score_ref[image, group * GROUP * slots : (group + 1) * GROUP * slots]
        part = transposed_times(score_grad, keys)
        if low:
            part = jnp.concatenate([jnp.zeros((part.shape[0], low), jnp.float32), part], axis=1)
        if high < features:
            part = jnp.concatenate(
                [part, jnp.zeros((part.shape[0], features - high), jnp.float32)], axis=1
            )
        parts.append(part)
    query_grad = functools.reduce(jnp.add, parts).astype(jnp.bfloat16)
    tile = tokens // out_sem.shape[0]
    copies = []
    for step in range(out_sem.shape[0]):
        rows = slice(step * tile, (step + 1) * tile)
        result[rows] = times_transposed(query_grad[rows], weight[...]).astype(jnp.bfloat16)
        copies.append(
            pltpu.make_async_copy(
                result.at[rows], out_ref.at[pl.ds(image * tokens + step * tile, tile)], out_sem.at[step]
            )
        )
        copies[-1].start()
    wait_all(copies)


def own_kernel(place_ref, mine, far, first_weight, second_weight, slope_ref, phrase_out, act_out, grad):
    join_halves(grad, place_ref[1], 0, [mine], [far])
    hidden_grad = times_transposed(grad[...], second_weight[...])
    act_out[...] = (hidden_grad * slope_ref[: act_out.shape[0]]).astype(jnp.bfloat16)
    phrase_out[...] = times_transposed(act_out[...], first_weight[...]).astype(jnp.bfloat16)


def weight_grad_kernel(planes, place_ref, *refs):
    mine, far = refs[:planes], refs[planes : 2 * planes]
    (
        second_weight,
        act_ref,
        slope_ref,
        hidden_ref,
        phrase_ref,
        second_out,
        first_out,
        encoded_grad,
        act_grad,
        second_grad,
        first_grad,
        out_sem,
    ) = refs[2 * planes :]
    join_halves(encoded_grad, place_ref[1], 0, mine, far)
    second_grad[...] = transposed_times(hidden_ref[...], encoded_grad[...])
    second_copy = pltpu.make_async_copy(second_grad, second_out, out_sem.at[0])
    second_copy.start()
    own = act_ref.shape[0]
    hidden_grad = times_transposed(encoded_grad[own:], second_weight[...])
    act_grad[:own] = act_ref[...]
    act_grad[own:] = (hidden_grad * slope_ref[own:]).astype(jnp.bfloat16)
    first_grad[...] = transposed_times(phrase_ref[...], act_grad[...])
    first_copy = pltpu.make_async_copy(first_grad, first_out, out_sem.at[1])
    first_copy.start()
    second_copy.wait()
    first_copy.wait()


def attention_grads(
    latents,
    out_grad,
    query_weight,
    key_rows,
    value_rows,
    region_first,
    region_last,
    phrase_counts,
    offset,
):
    images, tokens, features = latents.shape
    slot_count = key_rows.shape[1]
    head_count = H
    head_size = features // head_count
    score_scale = head_size ** (-0.5)
    queries = jnp.dot(
        latents.reshape(images * tokens, features), query_weight, preferred_element_type=jnp.float32
    ).astype(jnp.bfloat16)
    query_heads = queries.reshape(images, tokens, head_count, head_size)
    key_heads = key_rows.reshape(images, slot_count, head_count, head_size)
    value_heads = value_rows.reshape(images, slot_count, head_count, head_size)
    grad_heads = out_grad.reshape(images, tokens, head_count, head_size)
    scores = (
        jnp.einsum("ithd,iphd->ithp", query_heads, key_heads, preferred_element_type=jnp.float32)
        * score_scale
    )
    block_ids = (offset + jnp.arange(tokens, dtype=jnp.int32)) // BLOCK
    phrase_ids = jnp.arange(slot_count, dtype=jnp.int32)
    visible = (
        (phrase_ids[None, None, :] < phrase_counts[:, None, None])
        & (region_first[:, None, :] <= block_ids[None, :, None])
        & (block_ids[None, :, None] <= region_last[:, None, :])
    )
    scores = jnp.where(visible[:, :, None, :], scores, -jnp.inf)
    row_max = jnp.max(scores, axis=-1, keepdims=True)
    exponent = jnp.exp(scores - row_max)
    attn_probs = exponent / jnp.sum(exponent, axis=-1, keepdims=True)
    probs_low = attn_probs.astype(jnp.bfloat16)
    prob_grad = jnp.einsum(
        "ithd,iphd->ithp", grad_heads, value_heads, preferred_element_type=jnp.float32
    )
    inner_sum = jnp.sum(attn_probs * prob_grad, axis=-1, keepdims=True)
    score_grad = (attn_probs * (prob_grad - inner_sum) * score_scale).astype(jnp.bfloat16)
    query_grad = jnp.einsum(
        "ithp,iphd->ithd", score_grad, key_heads, preferred_element_type=jnp.float32
    ).astype(jnp.bfloat16)
    latent_grad = times_transposed(
        query_grad.reshape(images * tokens, features), query_weight
    ).astype(jnp.bfloat16)
    key_part = jnp.einsum(
        "ithp,ithd->iphd", score_grad, query_heads, preferred_element_type=jnp.float32
    ).reshape(images, slot_count, features)
    value_part = jnp.einsum(
        "ithp,ithd->iphd", probs_low, grad_heads, preferred_element_type=jnp.float32
    ).reshape(images, slot_count, features)
    return (latent_grad.reshape(images, tokens, features), key_part, value_part)


def plain(
    latents,
    out_grad,
    phrases,
    query_weight,
    key_weight,
    value_weight,
    first_weight,
    second_weight,
    region_first,
    region_last,
    phrase_counts,
):
    images, tokens, features = latents.shape
    slot_count = phrases.shape[1]
    shard_rows = first_weight.shape[0]
    col_start = lax.axis_index("seq") * shard_rows
    phrase_rows = phrases.reshape(images * slot_count, features)

    def own_cols(matrix):
        return lax.dynamic_slice_in_dim(matrix, col_start, shard_rows, 1)

    full_first, full_second, full_key, full_value = (
        lax.all_gather(first_weight, "seq", axis=0, tiled=True),
        lax.all_gather(second_weight, "seq", axis=0, tiled=True),
        lax.all_gather(key_weight, "seq", axis=0, tiled=True),
        lax.all_gather(value_weight, "seq", axis=0, tiled=True),
    )
    pre_act = jnp.dot(phrase_rows, full_first, preferred_element_type=jnp.float32)
    hidden = jax.nn.silu(pre_act).astype(jnp.bfloat16)
    encoded = jnp.dot(hidden, full_second, preferred_element_type=jnp.float32).astype(jnp.bfloat16)
    key_rows = jnp.dot(encoded, full_key, preferred_element_type=jnp.float32).astype(jnp.bfloat16)
    value_rows = jnp.dot(encoded, full_value, preferred_element_type=jnp.float32).astype(
        jnp.bfloat16
    )
    offset = lax.axis_index("seq") * tokens
    latent_grad, key_part, value_part = attention_grads(
        latents,
        out_grad,
        query_weight,
        key_rows.reshape(images, slot_count, features),
        value_rows.reshape(images, slot_count, features),
        region_first,
        region_last,
        phrase_counts,
        offset,
    )
    key_sum_grad, value_sum_grad = lax.psum((key_part, value_part), "seq")
    key_grad = key_sum_grad.astype(jnp.bfloat16).reshape(images * slot_count, features)
    value_grad = value_sum_grad.astype(jnp.bfloat16).reshape(images * slot_count, features)
    encoded_grad = (
        times_transposed(key_grad, full_key) + times_transposed(value_grad, full_value)
    ).astype(jnp.bfloat16)
    second_grad = transposed_times(own_cols(hidden), encoded_grad)
    hidden_grad = times_transposed(encoded_grad, full_second)
    act_grad = (hidden_grad * silu_slope(pre_act)).astype(jnp.bfloat16)
    first_grad = transposed_times(own_cols(phrase_rows), act_grad)
    phrase_grad = times_transposed(act_grad, full_first).astype(jnp.bfloat16)
    first_grad, second_grad = lax.psum((first_grad, second_grad), "dp")
    return (latent_grad, phrase_grad.reshape(images, slot_count, features), first_grad, second_grad)


def local(shards, planes, *args):
    shard_rows = args[6].shape[0]
    if shard_rows % 16:
        return plain(*args)
    return tiled(shards, planes, *args)


def tiled(
    shards,
    planes,
    latents,
    out_grad,
    phrases,
    query_weight,
    key_weight,
    value_weight,
    first_weight,
    second_weight,
    region_first,
    region_last,
    phrase_counts,
):
    images, tokens, features = latents.shape
    slots = phrases.shape[1]
    shard_rows = first_weight.shape[0]
    chips = shards // 2
    rows = images * slots
    half = rows // 2
    shard, plane = lax.axis_index("seq"), lax.axis_index("dp")
    core = shard % 2
    place = jnp.stack([shard // 2, core, plane % 2]).astype(jnp.int32)
    shape = jax.ShapeDtypeStruct

    def swap(array, distance):
        return lax.ppermute(array, "seq", [(i, i ^ distance) for i in range(shards)])

    def swap_by_plane(array, even, odd):
        pairs = [
            (p * shards + i, p * shards + (i ^ (2 * (odd if p % 2 else even))))
            for p in range(planes)
            for i in range(shards)
        ]
        return lax.ppermute(array, ("dp", "seq"), pairs)

    def chip_peers(array):
        return [swap(array, 2 * k) for k in range(1, chips)]

    def plane_swap(array, distance):
        return lax.ppermute(array, "dp", [(i, i ^ distance) for i in range(planes)])

    def plane_peers(array):
        return [plane_swap(array, k) for k in range(1, planes)]

    def after_all(parts, *others):
        return lax.optimization_barrier((*parts, *others))[: len(parts)]

    def after(array, *others):
        return lax.optimization_barrier((array, *others))[0]

    def with_other_core(blocks):
        return blocks + [swap(block, 1) for block in blocks]

    def total_of(parts):
        return functools.reduce(jnp.add, [part.astype(jnp.float32) for part in parts])

    def project_queries(tokens_in):
        return pl.pallas_call(
            query_kernel,
            out_shape=shape((images * tokens, features), jnp.bfloat16),
            grid=(images * tokens // 256,),
            in_specs=[
                pl.BlockSpec((256, features), lambda t: (t, 0)),
                pl.BlockSpec((features, features), lambda t: (0, 0)),
            ],
            out_specs=pl.BlockSpec((256, features), lambda t: (t, 0)),
            compiler_params=vmem(12),
            cost_estimate=pl.CostEstimate(
                flops=3 * 10**9, bytes_accessed=8 * 10**6, transcendentals=0
            ),
            name="queries",
        )(tokens_in.reshape(images * tokens, features), query_weight)

    phrase_rows = phrases.reshape(rows, features)
    bias = visible_bias(region_first, region_last, phrase_counts, shard * tokens, tokens)
    weight_shape = pltpu.VMEM((features, features), jnp.bfloat16)
    sum_shape = pltpu.VMEM((rows, features), jnp.float32)
    def join(parts, lengths, whole_rows):
        return pl.pallas_call(
            join_kernel,
            out_shape=[shape((whole_rows, features), jnp.bfloat16)] * lengths,
            in_specs=[VMEM] * len(parts),
            out_specs=[VMEM] * lengths,
            name="join",
        )(*parts)

    encoder, projector = join(
        [first_weight, second_weight, key_weight, value_weight], 2, 2 * shard_rows
    )
    if chips == 4:
        encoder_near = swap_by_plane(encoder, 1, 2)
        projector_near = swap_by_plane(projector, 2, 1)
        encoder_own, projector_own = swap(encoder, 1), swap(projector, 1)
        own_half = lax.dynamic_slice_in_dim(
            after(phrase_rows, encoder_own, projector_own), core * half, half, 0
        )
        plane_phrases = plane_peers(own_half)
        far_phrases = [swap(part, 1) for part in plane_phrases]
        encoder_next, projector_near, far_phrases, bias, place = lax.optimization_barrier(
            (encoder_near, projector_near, far_phrases, bias, place)
        )
        projector_third = swap_by_plane(projector, 1, 2)
        encoder_far = swap_by_plane(encoder_next, 2, 1)
        encoder_third = plane_swap(encoder_next, 1)
        key_near = projector_near[:shard_rows]
        queries = project_queries(after(latents, key_near))
        pairs = [swap(after(encoder_next, key_near), 1), swap(projector_near, 1)]
        key_far = swap_by_plane(after(key_near, projector_third), 1, 2)
        value_far = swap_by_plane(projector_third[shard_rows:], 2, 1)
        arrays = [encoder, encoder_near, projector, projector_near]
        arrays += [encoder_far, encoder_third, projector_third, key_far, value_far]
        arrays += [encoder_own, pairs[0], projector_own, pairs[1]]
        early = after_all([encoder_far, encoder_third], projector_third, queries)
        arrays += [swap(block, 1) for block in (*early, projector_third)]
        layout = {
            "first": (0, [(0, 0), (1, 0), (5, 0), (4, 0)]),
            "second": (0, [(i, shard_rows) for i in (0, 1, 5, 4)]),
            "key": (1, [(2, 0), (3, 0), (6, 0), (7, 0)]),
            "value": (1, [(2, shard_rows), (3, shard_rows), (6, shard_rows), (8, 0)]),
        }
    else:
        own_half = lax.dynamic_slice_in_dim(phrase_rows, core * half, half, 0)
        plane_phrases = plane_peers(own_half)
        far_phrases = [swap(part, 1) for part in plane_phrases]
        queries = project_queries(latents)
        arrays = [encoder] + chip_peers(encoder) + [projector] + chip_peers(projector)
        arrays += [swap(block, 1) for block in arrays]
        layout = {
            name: (0, [(first + k, offset) for k in range(chips)])
            for name, first, offset in (
                ("first", 0, 0),
                ("second", 0, shard_rows),
                ("key", chips, 0),
                ("value", chips, shard_rows),
            )
        }
    near_count = chips == 4 and 9 or len(arrays) // 2
    for name, (scheme, blocks) in layout.items():
        layout[name] = (scheme, blocks + [(near_count + i, offset) for i, offset in blocks])

    def weights(*names):
        used = sorted({i for name in names for i, _ in layout[name][1]})
        own_layout = {
            name: (layout[name][0], [(used.index(i), offset) for i, offset in layout[name][1]])
            for name in names
        }
        return [arrays[i] for i in used], {**own_layout, "arrays": len(used)}

    all_rows = planes * rows
    encoder_arrays, encoder_layout = weights("first", "second")
    encoded, slope, own_hidden, own_phrases, whole_first, whole_second = pl.pallas_call(
        functools.partial(encode_kernel, chips, planes, encoder_layout),
        out_shape=[
            shape((rows, features), jnp.bfloat16),
            shape((all_rows, features), jnp.float32),
            shape((all_rows, shard_rows), jnp.bfloat16),
            shape((all_rows, shard_rows), jnp.bfloat16),
            shape((features, features), jnp.bfloat16),
            shape((features, features), jnp.bfloat16),
        ],
        in_specs=[SMEM] + [VMEM] * (2 * planes - 1 + len(encoder_arrays)),
        out_specs=[VMEM] * 6,
        scratch_shapes=[pltpu.VMEM((all_rows, features), jnp.bfloat16)],
        compiler_params=vmem(18),
        cost_estimate=pl.CostEstimate(
            flops=10**6, bytes_accessed=10**4, transcendentals=0
        ),
        name="encode",
    )(place, phrase_rows, *plane_phrases, *far_phrases, *encoder_arrays)
    grads = out_grad.reshape(images * tokens, features)
    if chips == 4:
        *late, encoded = lax.optimization_barrier((*arrays[7:9], encoded))
        arrays[7:9] = late
        arrays += [swap(block, 1) for block in late]
    projector_arrays, projector_layout = weights("key", "value")
    key_rows, score_grad, grad_mine, grad_other = pl.pallas_call(
        functools.partial(attend_kernel, chips, images, projector_layout),
        out_shape=[
            shape((rows, features), jnp.bfloat16),
            shape((images, H * slots, tokens), jnp.bfloat16),
            shape((half, features), jnp.float32),
            shape((half, features), jnp.float32),
        ],
        in_specs=[SMEM] + [VMEM] * (len(projector_arrays) + 4),
        out_specs=[VMEM] * 4,
        scratch_shapes=[
            weight_shape,
            weight_shape,
            pltpu.VMEM((rows, features), jnp.bfloat16),
            sum_shape,
            sum_shape,
            sum_shape,
        ],
        compiler_params=vmem(28),
        cost_estimate=pl.CostEstimate(
            flops=10**10, bytes_accessed=12 * 10**6, transcendentals=10**6
        ),
        name="attend",
    )(place, encoded, *projector_arrays, queries, grads, bias)

    def latent_part(image, scores_in, whole=None):
        given = [] if whole is None else [whole]
        kernel = functools.partial(latent_kernel, image)
        return pl.pallas_call(
            kernel if whole is None else lambda _, *refs: kernel(*refs),
            out_shape=shape((images * tokens, features), jnp.bfloat16),
            in_specs=[ANY] * len(given) + [VMEM] * 3,
            out_specs=ANY,
            scratch_shapes=[
                pltpu.VMEM((tokens, features), jnp.bfloat16),
                pltpu.SemaphoreType.DMA((2,)),
            ],
            input_output_aliases={0: 0} if given else {},
            compiler_params=vmem(12),
            cost_estimate=pl.CostEstimate(
                flops=3 * 10**9, bytes_accessed=4 * 10**6, transcendentals=0
            ),
            name="latent",
        )(*given, scores_in, key_rows, query_weight)

    grad_pair = total_of([grad_mine, swap(grad_other, 1)]).astype(jnp.bfloat16)
    grad_own = total_of([grad_pair] + chip_peers(grad_pair)).astype(jnp.bfloat16)
    latent_grad = latent_part(0, score_grad)
    grad_own, latent_grad = lax.optimization_barrier((grad_own, latent_grad))
    for image in range(1, images):
        latent_grad = latent_part(image, score_grad, latent_grad)
    grad_mines = [grad_own] + plane_peers(grad_own)
    grad_fars = [swap(grad_own, 1)]
    phrase_grad, act_own = pl.pallas_call(
        own_kernel,
        out_shape=[shape((rows, features), jnp.bfloat16)] * 2,
        in_specs=[SMEM] + [VMEM] * 5,
        out_specs=[VMEM] * 2,
        scratch_shapes=[pltpu.VMEM((rows, features), jnp.bfloat16)],
        compiler_params=vmem(12),
        cost_estimate=pl.CostEstimate(flops=10**9, bytes_accessed=6 * 10**6, transcendentals=0),
        name="own_grads",
    )(place, grad_own, grad_fars[0], whole_first, whole_second, slope)
    grad_fars += [swap(part, 1) for part in after_all(grad_mines[1:], latent_grad, act_own)]
    second_grad, first_grad = pl.pallas_call(
        functools.partial(weight_grad_kernel, planes),
        out_shape=[
            shape((shard_rows, features), jnp.float32),
            shape((shard_rows, features), jnp.float32),
        ],
        in_specs=[SMEM] + [VMEM] * (2 * planes + 5),
        out_specs=[ANY, ANY],
        scratch_shapes=[
            pltpu.VMEM((all_rows, features), jnp.bfloat16),
            pltpu.VMEM((all_rows, features), jnp.bfloat16),
            pltpu.VMEM((shard_rows, features), jnp.float32),
            pltpu.VMEM((shard_rows, features), jnp.float32),
            pltpu.SemaphoreType.DMA((2,)),
        ],
        compiler_params=vmem(20),
        name="weight_grads",
    )(
        place,
        *grad_mines,
        *grad_fars,
        whole_second,
        act_own,
        slope,
        own_hidden,
        own_phrases,
    )
    return (
        latent_grad.reshape(images, tokens, features),
        phrase_grad.reshape(images, slots, features),
        first_grad,
        second_grad,
    )


def solution(mesh):
    shards, planes = mesh.shape["seq"], mesh.shape["dp"]
    in_specs = (
        P("dp", "seq", None),
        P("dp", "seq", None),
        P("dp", None, None),
        P(),
        P("seq", None),
        P("seq", None),
        P("seq", None),
        P("seq", None),
        P("dp", None),
        P("dp", None),
        P("dp"),
    )
    out_specs = (P("dp", "seq", None), P("dp", None, None), P("seq", None), P("seq", None))
    return jax.shard_map(
        functools.partial(local, shards, planes),
        mesh=mesh,
        in_specs=in_specs,
        out_specs=out_specs,
        check_vma=False,
    )
```

```python
import functools

import jax
import jax.numpy as jnp
from jax import lax
from jax.experimental import pallas as pl
from jax.experimental.pallas import tpu as pltpu
from jax.sharding import PartitionSpec as P

H = 16
BLOCK = 128
GROUP = 8
VMEM = pl.BlockSpec(memory_space=pltpu.VMEM)
SMEM = pl.BlockSpec(memory_space=pltpu.SMEM)
ANY = pl.BlockSpec(memory_space=pl.ANY)


def vmem(mebibytes):
    return pltpu.CompilerParams(vmem_limit_bytes=mebibytes * 1024 * 1024)


def silu_slope(pre_act):
    sigmoid = jax.nn.sigmoid(pre_act)
    return sigmoid * (1.0 + pre_act * (1.0 - sigmoid))


def contract(left_arg, right_arg, left_dim, right_dim):
    return lax.dot_general(
        left_arg,
        right_arg,
        (((left_dim,), (right_dim,)), ((), ())),
        preferred_element_type=jnp.float32,
    )


def times_transposed(left_arg, right_arg):
    return contract(left_arg, right_arg, 1, 1)


def transposed_times(left_arg, right_arg):
    return contract(left_arg, right_arg, 0, 0)


def split_times_transposed(left_arg, right_arg):
    rows = left_arg.shape[0]
    high = left_arg.astype(jnp.bfloat16)
    low = (left_arg - high.astype(jnp.float32)).astype(jnp.bfloat16)
    product = times_transposed(jnp.concatenate([high, low], axis=0), right_arg)
    return product[:rows] + product[rows:]


def visible_bias(region_first, region_last, phrase_counts, offset, tokens):
    block_ids = (offset + jnp.arange(tokens, dtype=jnp.int32)) // BLOCK
    phrase_ids = jnp.arange(region_first.shape[1], dtype=jnp.int32)
    visible = (
        (phrase_ids[None, :, None] < phrase_counts[:, None, None])
        & (region_first[:, :, None] <= block_ids[None, None, :])
        & (block_ids[None, None, :] <= region_last[:, :, None])
    )
    return jnp.where(visible, 0.0, -jnp.inf).astype(jnp.float32)


def window(group, head_size):
    start = group * GROUP * head_size
    return start // 128 * 128, -(-(start + GROUP * head_size) // 128) * 128


def own_columns(rows, group, head, head_size, low):
    first = (group * GROUP + head) * head_size - low
    column = lax.broadcasted_iota(jnp.int32, rows.shape, 1)
    return jnp.where((column >= first) & (column < first + head_size), rows, jnp.zeros_like(rows))


def block_diagonal(rows, group, head_size, low):
    return jnp.concatenate(
        [own_columns(rows, group, head, head_size, low) for head in range(GROUP)], axis=0
    )


def block_places(place_ref, scheme, chips):
    chip, core, odd = place_ref[0], place_ref[1], place_ref[2]
    steps = list(range(chips))
    if chips == 4:
        turn = odd if scheme == 0 else 1 - odd
        steps = [0, 1 + turn, 2 - turn, 3]
    return [2 * (chip ^ step) + other for other in (core, 1 - core) for step in steps]


def load_weight(name, layout, arrays, place_ref, chips, whole):
    scheme, blocks = layout[name]
    rows = whole.shape[0] // len(blocks)
    for (array, offset), place in zip(blocks, block_places(place_ref, scheme, chips)):
        whole[pl.ds(pl.multiple_of(place * rows, 16), rows)] = arrays[array][offset : offset + rows]


def project(left_arg, right_arg):
    return jnp.dot(left_arg, right_arg, preferred_element_type=jnp.float32)


def join_kernel(*refs):
    *parts, encoder_out, projector_out, sem = refs
    rows = parts[0].shape[0]
    copies = []
    for i, part in enumerate(parts):
        out = (encoder_out, projector_out)[i // 2].at[pl.ds(i % 2 * rows, rows)]
        copies.append(pltpu.make_async_copy(part, out, sem.at[i]))
        copies[-1].start()
    wait_all(copies)


def join_halves(out_ref, core, start, mine, far):
    half = mine[0].shape[0]
    for plane in range(len(mine)):
        first = start + plane * 2 * half
        out_ref[pl.ds(pl.multiple_of(first + core * half, 16), half)] = mine[plane][...]
        out_ref[pl.ds(pl.multiple_of(first + (1 - core) * half, 16), half)] = far[plane][...]


def wait_all(copies):
    for copy in copies:
        copy.wait()


def encode_kernel(chips, planes, layout, place_ref, phrase_ref, *refs):
    others = planes - 1
    mine, far = refs[:others], refs[others : 2 * others]
    arrays = refs[2 * others : 2 * others + layout["arrays"]]
    (
        encoded_out,
        slope_out,
        own_hidden_out,
        own_phrase_out,
        first_weight,
        second_weight,
        phrases,
    ) = refs[2 * others + layout["arrays"] :]
    own_rows = phrase_ref.shape[0]
    phrases[:own_rows] = phrase_ref[...]
    join_halves(phrases, place_ref[1], own_rows, mine, far)
    load_weight("first", layout, arrays, place_ref, chips, first_weight)
    load_weight("second", layout, arrays, place_ref, chips, second_weight)
    columns = own_phrase_out.shape[1]
    selected = lax.broadcasted_iota(jnp.int32, (phrases.shape[1], columns), 0)
    selected -= (2 * place_ref[0] + place_ref[1]) * columns
    select = selected == lax.broadcasted_iota(jnp.int32, selected.shape, 1)
    select = jnp.where(select, 1.0, 0.0).astype(jnp.bfloat16)
    own_phrase_out[...] = project(phrases[...], select).astype(jnp.bfloat16)
    pre_act = project(phrases[...], first_weight[...])
    sigmoid = jax.nn.sigmoid(pre_act)
    hidden = (pre_act * sigmoid).astype(jnp.bfloat16)
    slope_out[...] = sigmoid * (1.0 + pre_act * (1.0 - sigmoid))
    own_hidden_out[...] = project(hidden, select).astype(jnp.bfloat16)
    encoded_out[...] = project(hidden[:own_rows], second_weight[...]).astype(jnp.bfloat16)


def query_kernel(token_ref, weight_ref, out_ref):
    out_ref[...] = project(token_ref[...], weight_ref[...]).astype(jnp.bfloat16)


def head_parts(slots):
    return [slice(head * slots, (head + 1) * slots) for head in range(GROUP)]


def own_head_sum(full, group, head_size, low):
    slots = full.shape[0] // GROUP
    return functools.reduce(
        jnp.add,
        [
            own_columns(full[part], group, head, head_size, low)
            for head, part in enumerate(head_parts(slots))
        ],
    )


def attend_kernel(chips, images, layout, place_ref, encoded_ref, *refs):
    arrays = refs[: layout["arrays"]]
    (
        query,
        grad,
        bias_ref,
        key_out,
        score_out,
        mine_out,
        other_out,
        key_weight,
        value_weight,
        value_rows,
        key_sum,
        value_sum,
        total,
    ) = refs[layout["arrays"] :]
    own_rows = encoded_ref.shape[0]
    load_weight("key", layout, arrays, place_ref, chips, key_weight)
    load_weight("value", layout, arrays, place_ref, chips, value_weight)
    key_out[...] = project(encoded_ref[...], key_weight[...]).astype(jnp.bfloat16)
    value_rows[...] = project(encoded_ref[...], value_weight[...]).astype(jnp.bfloat16)

    slots = own_rows // images
    features = query.shape[1]
    tokens = query.shape[0] // images
    head_size = features // H
    scale = head_size ** (-0.5)
    key_sum[...] = jnp.zeros_like(key_sum)
    value_sum[...] = jnp.zeros_like(value_sum)
    for image in range(images):
        rows = pl.ds(image * slots, slots)
        here = pl.ds(image * tokens, tokens)
        bias = bias_ref[image]
        for group in range(H // GROUP):
            low, high = window(group, head_size)
            columns = pl.ds(low, high - low)
            keys = block_diagonal(key_out[rows, columns], group, head_size, low)
            values = block_diagonal(value_rows[rows, columns], group, head_size, low)
            queries = query[here, columns]
            grads = grad[here, columns]
            scores = times_transposed(keys, queries)
            prob_grad = times_transposed(values, grads)
            probs_low, score_grad = [], []
            for part in head_parts(slots):
                score = scores[part] * scale + bias
                exponent = jnp.exp(score - jnp.max(score, axis=0, keepdims=True))
                probs = exponent * (1.0 / jnp.sum(exponent, axis=0, keepdims=True))
                upstream = prob_grad[part]
                inner = jnp.sum(probs * upstream, axis=0, keepdims=True)
                probs_low.append(probs.astype(jnp.bfloat16))
                score_grad.append((probs * (upstream - inner) * scale).astype(jnp.bfloat16))
            probs_low = jnp.concatenate(probs_low, axis=0)
            score_grad = jnp.concatenate(score_grad, axis=0)
            score_out[image, pl.ds(group * GROUP * slots, GROUP * slots)] = score_grad
            key_sum[rows, columns] += own_head_sum(
                project(score_grad, queries), group, head_size, low
            )
            value_sum[rows, columns] += own_head_sum(
                project(probs_low, grads), group, head_size, low
            )
    total[...] = split_times_transposed(key_sum[...], key_weight[...]) + split_times_transposed(
        value_sum[...], value_weight[...]
    )
    core = place_ref[1]
    half = mine_out.shape[0]
    mine_out[...] = total[pl.ds(pl.multiple_of(core * half, 8), half)]
    other_out[...] = total[pl.ds(pl.multiple_of((1 - core) * half, 8), half)]


def latent_kernel(image, score_ref, key_ref, weight, out_ref, result, out_sem):
    slots, features = key_ref.shape[0] // score_ref.shape[0], weight.shape[0]
    tokens = score_ref.shape[2]
    head_size = features // H
    parts = []
    for group in range(H // GROUP):
        low, high = window(group, head_size)
        rows = key_ref[image * slots : (image + 1) * slots, low:high]
        keys = block_diagonal(rows, group, head_size, low)
        score_grad = score_ref[image, group * GROUP * slots : (group + 1) * GROUP * slots]
        part = transposed_times(score_grad, keys)
        if low:
            part = jnp.concatenate([jnp.zeros((part.shape[0], low), jnp.float32), part], axis=1)
        if high < features:
            part = jnp.concatenate(
                [part, jnp.zeros((part.shape[0], features - high), jnp.float32)], axis=1
            )
        parts.append(part)
    query_grad = functools.reduce(jnp.add, parts).astype(jnp.bfloat16)
    tile = tokens // out_sem.shape[0]
    copies = []
    for step in range(out_sem.shape[0]):
        rows = slice(step * tile, (step + 1) * tile)
        result[rows] = times_transposed(query_grad[rows], weight[...]).astype(jnp.bfloat16)
        copies.append(
            pltpu.make_async_copy(
                result.at[rows], out_ref.at[pl.ds(image * tokens + step * tile, tile)], out_sem.at[step]
            )
        )
        copies[-1].start()
    wait_all(copies)


def own_kernel(place_ref, mine, far, first_weight, second_weight, slope_ref, phrase_out, act_out, grad):
    join_halves(grad, place_ref[1], 0, [mine], [far])
    hidden_grad = times_transposed(grad[...], second_weight[...])
    act_out[...] = (hidden_grad * slope_ref[: act_out.shape[0]]).astype(jnp.bfloat16)
    phrase_out[...] = times_transposed(act_out[...], first_weight[...]).astype(jnp.bfloat16)


def weight_grad_kernel(planes, place_ref, *refs):
    mine, far = refs[:planes], refs[planes : 2 * planes]
    (
        second_weight,
        act_ref,
        slope_ref,
        hidden_ref,
        phrase_ref,
        second_out,
        first_out,
        encoded_grad,
        act_grad,
        second_grad,
        first_grad,
        out_sem,
    ) = refs[2 * planes :]
    join_halves(encoded_grad, place_ref[1], 0, mine, far)
    second_grad[...] = transposed_times(hidden_ref[...], encoded_grad[...])
    second_copy = pltpu.make_async_copy(second_grad, second_out, out_sem.at[0])
    second_copy.start()
    own = act_ref.shape[0]
    hidden_grad = times_transposed(encoded_grad[own:], second_weight[...])
    act_grad[:own] = act_ref[...]
    act_grad[own:] = (hidden_grad * slope_ref[own:]).astype(jnp.bfloat16)
    first_grad[...] = transposed_times(phrase_ref[...], act_grad[...])
    first_copy = pltpu.make_async_copy(first_grad, first_out, out_sem.at[1])
    first_copy.start()
    second_copy.wait()
    first_copy.wait()


def attention_grads(
    latents,
    out_grad,
    query_weight,
    key_rows,
    value_rows,
    region_first,
    region_last,
    phrase_counts,
    offset,
):
    images, tokens, features = latents.shape
    slot_count = key_rows.shape[1]
    head_count = H
    head_size = features // head_count
    score_scale = head_size ** (-0.5)
    queries = jnp.dot(
        latents.reshape(images * tokens, features), query_weight, preferred_element_type=jnp.float32
    ).astype(jnp.bfloat16)
    query_heads = queries.reshape(images, tokens, head_count, head_size)
    key_heads = key_rows.reshape(images, slot_count, head_count, head_size)
    value_heads = value_rows.reshape(images, slot_count, head_count, head_size)
    grad_heads = out_grad.reshape(images, tokens, head_count, head_size)
    scores = (
        jnp.einsum("ithd,iphd->ithp", query_heads, key_heads, preferred_element_type=jnp.float32)
        * score_scale
    )
    block_ids = (offset + jnp.arange(tokens, dtype=jnp.int32)) // BLOCK
    phrase_ids = jnp.arange(slot_count, dtype=jnp.int32)
    visible = (
        (phrase_ids[None, None, :] < phrase_counts[:, None, None])
        & (region_first[:, None, :] <= block_ids[None, :, None])
        & (block_ids[None, :, None] <= region_last[:, None, :])
    )
    scores = jnp.where(visible[:, :, None, :], scores, -jnp.inf)
    row_max = jnp.max(scores, axis=-1, keepdims=True)
    exponent = jnp.exp(scores - row_max)
    attn_probs = exponent / jnp.sum(exponent, axis=-1, keepdims=True)
    probs_low = attn_probs.astype(jnp.bfloat16)
    prob_grad = jnp.einsum(
        "ithd,iphd->ithp", grad_heads, value_heads, preferred_element_type=jnp.float32
    )
    inner_sum = jnp.sum(attn_probs * prob_grad, axis=-1, keepdims=True)
    score_grad = (attn_probs * (prob_grad - inner_sum) * score_scale).astype(jnp.bfloat16)
    query_grad = jnp.einsum(
        "ithp,iphd->ithd", score_grad, key_heads, preferred_element_type=jnp.float32
    ).astype(jnp.bfloat16)
    latent_grad = times_transposed(
        query_grad.reshape(images * tokens, features), query_weight
    ).astype(jnp.bfloat16)
    key_part = jnp.einsum(
        "ithp,ithd->iphd", score_grad, query_heads, preferred_element_type=jnp.float32
    ).reshape(images, slot_count, features)
    value_part = jnp.einsum(
        "ithp,ithd->iphd", probs_low, grad_heads, preferred_element_type=jnp.float32
    ).reshape(images, slot_count, features)
    return (latent_grad.reshape(images, tokens, features), key_part, value_part)


def plain(
    latents,
    out_grad,
    phrases,
    query_weight,
    key_weight,
    value_weight,
    first_weight,
    second_weight,
    region_first,
    region_last,
    phrase_counts,
):
    images, tokens, features = latents.shape
    slot_count = phrases.shape[1]
    shard_rows = first_weight.shape[0]
    col_start = lax.axis_index("seq") * shard_rows
    phrase_rows = phrases.reshape(images * slot_count, features)

    def own_cols(matrix):
        return lax.dynamic_slice_in_dim(matrix, col_start, shard_rows, 1)

    full_first, full_second, full_key, full_value = (
        lax.all_gather(first_weight, "seq", axis=0, tiled=True),
        lax.all_gather(second_weight, "seq", axis=0, tiled=True),
        lax.all_gather(key_weight, "seq", axis=0, tiled=True),
        lax.all_gather(value_weight, "seq", axis=0, tiled=True),
    )
    pre_act = jnp.dot(phrase_rows, full_first, preferred_element_type=jnp.float32)
    hidden = jax.nn.silu(pre_act).astype(jnp.bfloat16)
    encoded = jnp.dot(hidden, full_second, preferred_element_type=jnp.float32).astype(jnp.bfloat16)
    key_rows = jnp.dot(encoded, full_key, preferred_element_type=jnp.float32).astype(jnp.bfloat16)
    value_rows = jnp.dot(encoded, full_value, preferred_element_type=jnp.float32).astype(
        jnp.bfloat16
    )
    offset = lax.axis_index("seq") * tokens
    latent_grad, key_part, value_part = attention_grads(
        latents,
        out_grad,
        query_weight,
        key_rows.reshape(images, slot_count, features),
        value_rows.reshape(images, slot_count, features),
        region_first,
        region_last,
        phrase_counts,
        offset,
    )
    key_sum_grad, value_sum_grad = lax.psum((key_part, value_part), "seq")
    key_grad = key_sum_grad.astype(jnp.bfloat16).reshape(images * slot_count, features)
    value_grad = value_sum_grad.astype(jnp.bfloat16).reshape(images * slot_count, features)
    encoded_grad = (
        times_transposed(key_grad, full_key) + times_transposed(value_grad, full_value)
    ).astype(jnp.bfloat16)
    second_grad = transposed_times(own_cols(hidden), encoded_grad)
    hidden_grad = times_transposed(encoded_grad, full_second)
    act_grad = (hidden_grad * silu_slope(pre_act)).astype(jnp.bfloat16)
    first_grad = transposed_times(own_cols(phrase_rows), act_grad)
    phrase_grad = times_transposed(act_grad, full_first).astype(jnp.bfloat16)
    first_grad, second_grad = lax.psum((first_grad, second_grad), "dp")
    return (latent_grad, phrase_grad.reshape(images, slot_count, features), first_grad, second_grad)


def local(shards, planes, *args):
    shard_rows = args[6].shape[0]
    if shard_rows % 16:
        return plain(*args)
    return tiled(shards, planes, *args)


def tiled(
    shards,
    planes,
    latents,
    out_grad,
    phrases,
    query_weight,
    key_weight,
    value_weight,
    first_weight,
    second_weight,
    region_first,
    region_last,
    phrase_counts,
):
    images, tokens, features = latents.shape
    slots = phrases.shape[1]
    shard_rows = first_weight.shape[0]
    chips = shards // 2
    rows = images * slots
    half = rows // 2
    shard, plane = lax.axis_index("seq"), lax.axis_index("dp")
    core = shard % 2
    place = jnp.stack([shard // 2, core, plane % 2]).astype(jnp.int32)
    shape = jax.ShapeDtypeStruct

    def swap(array, distance):
        return lax.ppermute(array, "seq", [(i, i ^ distance) for i in range(shards)])

    def swap_by_plane(array, even, odd):
        pairs = [
            (p * shards + i, p * shards + (i ^ (2 * (odd if p % 2 else even))))
            for p in range(planes)
            for i in range(shards)
        ]
        return lax.ppermute(array, ("dp", "seq"), pairs)

    def chip_peers(array):
        return [swap(array, 2 * k) for k in range(1, chips)]

    def plane_swap(array, distance):
        return lax.ppermute(array, "dp", [(i, i ^ distance) for i in range(planes)])

    def plane_peers(array):
        return [plane_swap(array, k) for k in range(1, planes)]

    def after_all(parts, *others):
        return lax.optimization_barrier((*parts, *others))[: len(parts)]

    def after(array, *others):
        return lax.optimization_barrier((array, *others))[0]

    def with_other_core(blocks):
        return blocks + [swap(block, 1) for block in blocks]

    def total_of(parts):
        return functools.reduce(jnp.add, [part.astype(jnp.float32) for part in parts])

    def project_queries(tokens_in):
        return pl.pallas_call(
            query_kernel,
            out_shape=shape((images * tokens, features), jnp.bfloat16),
            grid=(images * tokens // 256,),
            in_specs=[
                pl.BlockSpec((256, features), lambda t: (t, 0)),
                pl.BlockSpec((features, features), lambda t: (0, 0)),
            ],
            out_specs=pl.BlockSpec((256, features), lambda t: (t, 0)),
            compiler_params=vmem(12),
            cost_estimate=pl.CostEstimate(
                flops=3 * 10**9, bytes_accessed=8 * 10**6, transcendentals=0
            ),
            name="queries",
        )(tokens_in.reshape(images * tokens, features), query_weight)

    phrase_rows = phrases.reshape(rows, features)
    bias = visible_bias(region_first, region_last, phrase_counts, shard * tokens, tokens)
    weight_shape = pltpu.VMEM((features, features), jnp.bfloat16)
    sum_shape = pltpu.VMEM((rows, features), jnp.float32)
    def join(parts, lengths, whole_rows):
        return pl.pallas_call(
            join_kernel,
            out_shape=[shape((whole_rows, features), jnp.bfloat16)] * lengths,
            in_specs=[ANY] * len(parts),
            out_specs=[VMEM] * lengths,
            scratch_shapes=[pltpu.SemaphoreType.DMA((len(parts),))],
            name="join",
        )(*parts)

    encoder, projector = join(
        [first_weight, second_weight, key_weight, value_weight], 2, 2 * shard_rows
    )
    if chips == 4:
        encoder_near = swap_by_plane(encoder, 1, 2)
        projector_near = swap_by_plane(projector, 2, 1)
        encoder_own, projector_own = swap(encoder, 1), swap(projector, 1)
        own_half = lax.dynamic_slice_in_dim(
            after(phrase_rows, encoder_own, projector_own), core * half, half, 0
        )
        plane_phrases = plane_peers(own_half)
        far_phrases = [swap(part, 1) for part in plane_phrases]
        encoder_next, projector_near, far_phrases, bias, place = lax.optimization_barrier(
            (encoder_near, projector_near, far_phrases, bias, place)
        )
        projector_third = swap_by_plane(projector, 1, 2)
        encoder_far = swap_by_plane(encoder_next, 2, 1)
        encoder_third = plane_swap(encoder_next, 1)
        key_near = projector_near[:shard_rows]
        queries = project_queries(after(latents, key_near))
        pairs = [swap(after(encoder_next, key_near), 1), swap(projector_near, 1)]
        key_far = swap_by_plane(after(key_near, projector_third), 1, 2)
        value_far = swap_by_plane(projector_third[shard_rows:], 2, 1)
        arrays = [encoder, encoder_near, projector, projector_near]
        arrays += [encoder_far, encoder_third, projector_third, key_far, value_far]
        arrays += [encoder_own, pairs[0], projector_own, pairs[1]]
        early = after_all([encoder_far, encoder_third], projector_third, queries)
        arrays += [swap(block, 1) for block in (*early, projector_third)]
        layout = {
            "first": (0, [(0, 0), (1, 0), (5, 0), (4, 0)]),
            "second": (0, [(i, shard_rows) for i in (0, 1, 5, 4)]),
            "key": (1, [(2, 0), (3, 0), (6, 0), (7, 0)]),
            "value": (1, [(2, shard_rows), (3, shard_rows), (6, shard_rows), (8, 0)]),
        }
    else:
        own_half = lax.dynamic_slice_in_dim(phrase_rows, core * half, half, 0)
        plane_phrases = plane_peers(own_half)
        far_phrases = [swap(part, 1) for part in plane_phrases]
        queries = project_queries(latents)
        arrays = [encoder] + chip_peers(encoder) + [projector] + chip_peers(projector)
        arrays += [swap(block, 1) for block in arrays]
        layout = {
            name: (0, [(first + k, offset) for k in range(chips)])
            for name, first, offset in (
                ("first", 0, 0),
                ("second", 0, shard_rows),
                ("key", chips, 0),
                ("value", chips, shard_rows),
            )
        }
    near_count = chips == 4 and 9 or len(arrays) // 2
    for name, (scheme, blocks) in layout.items():
        layout[name] = (scheme, blocks + [(near_count + i, offset) for i, offset in blocks])

    def weights(*names):
        used = sorted({i for name in names for i, _ in layout[name][1]})
        own_layout = {
            name: (layout[name][0], [(used.index(i), offset) for i, offset in layout[name][1]])
            for name in names
        }
        return [arrays[i] for i in used], {**own_layout, "arrays": len(used)}

    all_rows = planes * rows
    encoder_arrays, encoder_layout = weights("first", "second")
    encoded, slope, own_hidden, own_phrases, whole_first, whole_second = pl.pallas_call(
        functools.partial(encode_kernel, chips, planes, encoder_layout),
        out_shape=[
            shape((rows, features), jnp.bfloat16),
            shape((all_rows, features), jnp.float32),
            shape((all_rows, shard_rows), jnp.bfloat16),
            shape((all_rows, shard_rows), jnp.bfloat16),
            shape((features, features), jnp.bfloat16),
            shape((features, features), jnp.bfloat16),
        ],
        in_specs=[SMEM] + [VMEM] * (2 * planes - 1 + len(encoder_arrays)),
        out_specs=[VMEM] * 6,
        scratch_shapes=[pltpu.VMEM((all_rows, features), jnp.bfloat16)],
        compiler_params=vmem(18),
        cost_estimate=pl.CostEstimate(
            flops=10**6, bytes_accessed=10**4, transcendentals=0
        ),
        name="encode",
    )(place, phrase_rows, *plane_phrases, *far_phrases, *encoder_arrays)
    grads = out_grad.reshape(images * tokens, features)
    if chips == 4:
        *late, encoded = lax.optimization_barrier((*arrays[7:9], encoded))
        arrays[7:9] = late
        arrays += [swap(block, 1) for block in late]
    projector_arrays, projector_layout = weights("key", "value")
    key_rows, score_grad, grad_mine, grad_other = pl.pallas_call(
        functools.partial(attend_kernel, chips, images, projector_layout),
        out_shape=[
            shape((rows, features), jnp.bfloat16),
            shape((images, H * slots, tokens), jnp.bfloat16),
            shape((half, features), jnp.float32),
            shape((half, features), jnp.float32),
        ],
        in_specs=[SMEM] + [VMEM] * (len(projector_arrays) + 4),
        out_specs=[VMEM] * 4,
        scratch_shapes=[
            weight_shape,
            weight_shape,
            pltpu.VMEM((rows, features), jnp.bfloat16),
            sum_shape,
            sum_shape,
            sum_shape,
        ],
        compiler_params=vmem(28),
        cost_estimate=pl.CostEstimate(
            flops=10**10, bytes_accessed=12 * 10**6, transcendentals=10**6
        ),
        name="attend",
    )(place, encoded, *projector_arrays, queries, grads, bias)

    def latent_part(image, scores_in, whole=None):
        given = [] if whole is None else [whole]
        kernel = functools.partial(latent_kernel, image)
        return pl.pallas_call(
            kernel if whole is None else lambda _, *refs: kernel(*refs),
            out_shape=shape((images * tokens, features), jnp.bfloat16),
            in_specs=[ANY] * len(given) + [VMEM] * 3,
            out_specs=ANY,
            scratch_shapes=[
                pltpu.VMEM((tokens, features), jnp.bfloat16),
                pltpu.SemaphoreType.DMA((2,)),
            ],
            input_output_aliases={0: 0} if given else {},
            compiler_params=vmem(12),
            cost_estimate=pl.CostEstimate(
                flops=3 * 10**9, bytes_accessed=4 * 10**6, transcendentals=0
            ),
            name="latent",
        )(*given, scores_in, key_rows, query_weight)

    grad_pair = total_of([grad_mine, swap(grad_other, 1)]).astype(jnp.bfloat16)
    grad_own = total_of([grad_pair] + chip_peers(grad_pair)).astype(jnp.bfloat16)
    latent_grad = latent_part(0, score_grad)
    grad_own, latent_grad = lax.optimization_barrier((grad_own, latent_grad))
    for image in range(1, images):
        latent_grad = latent_part(image, score_grad, latent_grad)
    grad_mines = [grad_own] + plane_peers(grad_own)
    grad_fars = [swap(grad_own, 1)]
    phrase_grad, act_own = pl.pallas_call(
        own_kernel,
        out_shape=[shape((rows, features), jnp.bfloat16)] * 2,
        in_specs=[SMEM] + [VMEM] * 5,
        out_specs=[VMEM] * 2,
        scratch_shapes=[pltpu.VMEM((rows, features), jnp.bfloat16)],
        compiler_params=vmem(12),
        cost_estimate=pl.CostEstimate(flops=10**9, bytes_accessed=6 * 10**6, transcendentals=0),
        name="own_grads",
    )(place, grad_own, grad_fars[0], whole_first, whole_second, slope)
    grad_fars += [swap(part, 1) for part in after_all(grad_mines[1:], latent_grad, act_own)]
    second_grad, first_grad = pl.pallas_call(
        functools.partial(weight_grad_kernel, planes),
        out_shape=[
            shape((shard_rows, features), jnp.float32),
            shape((shard_rows, features), jnp.float32),
        ],
        in_specs=[SMEM] + [VMEM] * (2 * planes + 5),
        out_specs=[ANY, ANY],
        scratch_shapes=[
            pltpu.VMEM((all_rows, features), jnp.bfloat16),
            pltpu.VMEM((all_rows, features), jnp.bfloat16),
            pltpu.VMEM((shard_rows, features), jnp.float32),
            pltpu.VMEM((shard_rows, features), jnp.float32),
            pltpu.SemaphoreType.DMA((2,)),
        ],
        compiler_params=vmem(20),
        name="weight_grads",
    )(
        place,
        *grad_mines,
        *grad_fars,
        whole_second,
        act_own,
        slope,
        own_hidden,
        own_phrases,
    )
    return (
        latent_grad.reshape(images, tokens, features),
        phrase_grad.reshape(images, slots, features),
        first_grad,
        second_grad,
    )


def solution(mesh):
    shards, planes = mesh.shape["seq"], mesh.shape["dp"]
    in_specs = (
        P("dp", "seq", None),
        P("dp", "seq", None),
        P("dp", None, None),
        P(),
        P("seq", None),
        P("seq", None),
        P("seq", None),
        P("seq", None),
        P("dp", None),
        P("dp", None),
        P("dp"),
    )
    out_specs = (P("dp", "seq", None), P("dp", None, None), P("seq", None), P("seq", None))
    return jax.shard_map(
        functools.partial(local, shards, planes),
        mesh=mesh,
        in_specs=in_specs,
        out_specs=out_specs,
        check_vma=False,
    )
```
